256 devices in a mesh: seq: 64 (over z, x, core), head: 4 (over y).
Axes of the slice: x: 4, y: 4, z: 8, core: 2. Of those that a mesh axis runs over, the one named last changes fastest.
Arguments:
- inputs: bfloat16 [16384, 8192], P(('seq', 'head')), may hold values from -6 to 6
- gate: bfloat16 [16384, 8192], P('seq', 'head'), may hold values from -40 to 40
- in_b: bfloat16 [16384, 128], P('seq'), may hold values from -4 to 4
- in_c: bfloat16 [16384, 128], P('seq'), may hold values from -4 to 4
- log_decay: float32 [128, 16384], P('head', 'seq'), may hold values from -1 to 0
- step_size: float32 [128, 16384], P('head', 'seq'), may hold values from 0 to 1
- importance: float32 [16384], P('seq'), may hold values from 0.2 to 2
- skip: float32 [128], P('head'), may hold values from 0.5 to 1.5
- norm_gain: float32 [8192], P('head'), may hold values from 0.25 to 1.75
Outputs:
- outputs: bfloat16 [16384, 8192], P('seq', 'head')
The draws below stay inside these ranges and needn't reach their ends.
All inputs are finite; a program needn't handle non-finite values.
Results may differ from the reference program's by a relative error of at most 0.0055.
Values may be sent and summed in bfloat16 or wider, within the bound.
No kernel may reach another device: no remote copies, remote signals or barrier semaphores. Data moves between devices by JAX's collectives and lax.ppermute only.
A program may use at most 192 MiB of HBM per device.

```python
import math
import jax
import jax.numpy as jnp
from jax import lax

HEADS = 128
HEAD_DIM = 64
STATE = 128
STRETCH = 256
TOKENS = 16384


def decay_rates(key):
    fast_key, pick_key, slow_key = jax.random.split(jax.random.fold_in(key, 5), 3)
    share = 0.5
    chosen = jax.random.uniform(pick_key, (HEADS,)) < share
    fast_rate = jnp.exp(jax.random.uniform(fast_key, (HEADS,), minval=jnp.log(1.0 / 50.0), maxval=jnp.log(1.0 / 30.0)))
    slow_rate = jnp.exp(jax.random.uniform(slow_key, (HEADS,), minval=jnp.log(6.0), maxval=jnp.log(16.0))) / TOKENS
    slow_rate = jnp.minimum(slow_rate, 0.125)
    return jnp.where(chosen, fast_rate, slow_rate)


def draw_log_decay(key, part):
    forgetting_rates = decay_rates(key)
    rough_key, place_key, offset_key, depth_key = jax.random.split(jax.random.fold_in(key, 9), 4)
    rough_guess_value = jnp.exp(jax.random.uniform(rough_key, (HEADS, TOKENS), minval=jnp.log(0.5), maxval=jnp.log(2.0)))
    first_index_point = jax.random.randint(place_key, (HEADS, 1), 0, TOKENS)
    final_index_point = (first_index_point + 1 + jax.random.randint(offset_key, (HEADS, 1), 0, TOKENS - 1)) % TOKENS
    nesting_tiers = jnp.log(jax.random.uniform(depth_key, (HEADS, 2), minval=0.5, maxval=0.8))
    sequence_indices = jnp.arange(TOKENS)[None, :]
    episode_spans_list = jnp.where(sequence_indices == first_index_point, nesting_tiers[:, 0:1], 0.0)
    episode_spans_list = episode_spans_list + jnp.where(sequence_indices == final_index_point, nesting_tiers[:, 1:2], 0.0)
    return (-forgetting_rates[:, None] * rough_guess_value + episode_spans_list).astype(jnp.float32)


def draw_step_size(key, part):
    forgetting_rates = decay_rates(key)
    rough_key = jax.random.fold_in(key, 13)
    rough_guess_value = jnp.exp(jax.random.uniform(rough_key, (HEADS, TOKENS), minval=jnp.log(0.5), maxval=jnp.log(2.0)))
    return (jnp.sqrt(2.0 * forgetting_rates)[:, None] * rough_guess_value).astype(jnp.float32)


def draw_gate(key, part):
    features = HEADS * HEAD_DIM
    column_key, value_key = jax.random.split(jax.random.fold_in(key, 17))
    placing = jnp.arange(features).astype(jnp.float32) / features
    scales = jnp.exp(jnp.log(3.0) * placing + jax.random.uniform(column_key, (features,), minval=0.0, maxval=jnp.log(3.3)))
    values = jnp.clip(jax.random.normal(value_key, (TOKENS, features)), -4.0, 4.0)
    return (values * scales[None, :]).astype(jnp.bfloat16)


def block_scale(key, dims, shards, low, high):
    factor_of, own = 1.0, jax.random.fold_in(key, 6)
    for position, shards_of in shards:
        draws = jnp.exp(jax.random.uniform(jax.random.fold_in(own, position), (shards_of,), jnp.float32, low / len(shards), high / len(shards)))
        factor_of = factor_of * jnp.repeat(draws, dims[position] // shards_of).reshape([-1 if axis == position else 1 for axis in range(len(dims))])
    return factor_of


def normal_values(key, shape, scale, limit, cuts=(), held_as=jnp.bfloat16):
    drawn = jax.random.normal(key, shape, jnp.float32) * scale
    if len(cuts) > 0:
        drawn = block_scale(key, shape, cuts, -0.22, 0.18) * drawn
    return jnp.clip(drawn, min=-limit, max=limit).astype(held_as)


def setup_inputs(seed: int = 0) -> dict:
    arg_keys = jax.random.split(jax.random.key(seed), 10)
    inputs = normal_values(arg_keys[0], (TOKENS, HEADS * HEAD_DIM), 1.0, 6.0, ((0, 256),))
    gate = draw_gate(jax.random.fold_in(arg_keys[9], 71), 0)
    in_b = normal_values(arg_keys[2], (TOKENS, STATE), 0.3, 4.0, ((0, 64),))
    in_c = normal_values(arg_keys[3], (TOKENS, STATE), 0.3, 4.0, ((0, 64),))
    log_decay = draw_log_decay(jax.random.fold_in(arg_keys[9], 71), 0)
    step_size = draw_step_size(jax.random.fold_in(arg_keys[9], 71), 0)
    importance = jnp.clip(jnp.exp(math.log(2.0) - 2.3025851 * jax.random.uniform(arg_keys[6], (TOKENS,), jnp.float32) ** block_scale(arg_keys[6], (TOKENS,), ((0, 64),), -0.2, 0.2)), 0.2, 2.0)
    skip = jnp.clip(0.5 + 1.0 * jax.random.uniform(arg_keys[7], (HEADS,), jnp.float32) ** block_scale(arg_keys[7], (HEADS,), ((0, 4),), -0.2, 0.2), 0.5, 1.5)
    norm_gain = jnp.clip(1.0 + 0.15 * jax.random.normal(arg_keys[8], (HEADS * HEAD_DIM,), jnp.float32), 0.25, 1.75)
    return dict(inputs=inputs, gate=gate, in_b=in_b, in_c=in_c, log_decay=log_decay, step_size=step_size, importance=importance, skip=skip, norm_gain=norm_gain)


epsilon = 1e-05

def block_terms(scaled_in, b_rows, c_rows, log_rows):
    cumulative = jnp.cumsum(log_rows, axis=1)
    length = log_rows.shape[1]
    later = jnp.arange(length)[:, None] >= jnp.arange(length)[None, :]
    scores = jnp.dot(c_rows, b_rows.T, preferred_element_type=jnp.float32)
    spread = cumulative[:, :, None] - cumulative[:, None, :]
    raw_weights = jnp.where(later[None], scores[None] * jnp.exp(jnp.where(later[None], spread, 0.0)), 0.0)
    weights = lax.optimization_barrier(raw_weights.astype(jnp.bfloat16))
    within = jnp.einsum('hts,shp->thp', weights.astype(jnp.float32), scaled_in.astype(jnp.float32))
    tail = jnp.exp(cumulative[:, -1:] - cumulative)
    decayed = lax.optimization_barrier((b_rows.astype(jnp.float32)[None, :, :] * tail[:, :, None]).astype(jnp.bfloat16))
    local_state = jnp.einsum('hsn,shp->hpn', decayed.astype(jnp.float32), scaled_in.astype(jnp.float32))
    return (within, cumulative, local_state)

def reference(inputs, gate, in_b, in_c, log_decay, step_size, importance, skip, norm_gain):
    block_count = TOKENS // STRETCH
    features = HEADS * HEAD_DIM

    def advance(entering, pieces):
        input_rows, gate_rows, b_rows, c_rows, log_rows, step_rows, weight_rows = pieces
        channels = input_rows.astype(jnp.float32).reshape(STRETCH, HEADS, HEAD_DIM)
        scaled_raw = channels * step_rows.T[:, :, None] * weight_rows[:, None, None]
        scaled_in = lax.optimization_barrier(scaled_raw.astype(jnp.bfloat16))
        within, cumulative, local_state = block_terms(scaled_in, b_rows, c_rows, log_rows)
        rounded = lax.optimization_barrier(entering.astype(jnp.bfloat16))
        carried = jnp.einsum('tn,hpn->thp', c_rows.astype(jnp.float32), rounded.astype(jnp.float32))
        carried = carried * jnp.exp(cumulative).T[:, :, None]
        mixed = within + carried + skip[None, :, None] * channels
        gated = mixed.reshape(STRETCH, features) * jax.nn.silu(gate_rows.astype(jnp.float32))
        meansq = lax.optimization_barrier(jnp.mean(gated * gated, axis=1, keepdims=True))
        out_rows = (gated * lax.rsqrt(meansq + epsilon) * norm_gain[None, :]).astype(jnp.bfloat16)
        following = jnp.exp(cumulative[:, -1])[:, None, None] * entering + local_state
        return (following, out_rows)
    pieces = (inputs.reshape(block_count, STRETCH, features), gate.reshape(block_count, STRETCH, features), in_b.reshape(block_count, STRETCH, STATE), in_c.reshape(block_count, STRETCH, STATE), log_decay.reshape(HEADS, block_count, STRETCH).transpose(1, 0, 2), step_size.reshape(HEADS, block_count, STRETCH).transpose(1, 0, 2), importance.reshape(block_count, STRETCH))
    start = jnp.zeros((HEADS, HEAD_DIM, STATE), jnp.float32)
    final_state, out_blocks = lax.scan(advance, start, pieces)
    return out_blocks.reshape(TOKENS, features)
```

```python
import functools

import jax
import jax.numpy as jnp
from jax import lax
from jax.experimental import pallas as pl
from jax.experimental.pallas import tpu as pltpu
from jax.sharding import Mesh, PartitionSpec as P

HEADS = 128
HEAD_DIM = 64
STATE = 128
STRETCH = 256
epsilon = 1e-05

F32 = jnp.float32
BF16 = jnp.bfloat16
HERE = 32
FEATS = HERE * HEAD_DIM
HALF = FEATS // 2
PART = HALF // 4
LOGS = 16


def kernel_call(body, outs, *args, scratch=(), flops=0, bytes_accessed=0):
    vmem = pl.BlockSpec(memory_space=pltpu.VMEM)
    return pl.pallas_call(
        body,
        out_shape=[jax.ShapeDtypeStruct(s, d) for s, d in outs],
        in_specs=[vmem] * len(args),
        out_specs=[vmem] * len(outs),
        scratch_shapes=[pltpu.VMEM(s, d) for s, d in scratch],
        compiler_params=pltpu.CompilerParams(vmem_limit_bytes=40 * 1024 * 1024),
        cost_estimate=pl.CostEstimate(
            flops=flops, bytes_accessed=bytes_accessed, transcendentals=0
        ),
    )(*args)


def three_terms(v):
    hi = v.astype(BF16).astype(F32)
    rest = v - hi
    mid = rest.astype(BF16).astype(F32)
    return hi, mid, rest - mid


def pick(index, first, second):
    return jnp.where(jnp.full(first.shape, index, jnp.int32) == 0, first, second)


def place(axis, step, size):
    return lax.rem(lax.axis_index(axis) + (step + size), size)


def log_block(row):
    hi, mid, lo = three_terms(row)
    at = lax.broadcasted_iota(jnp.int32, (LOGS, row.shape[1]), 0)
    return jnp.where(at == 0, hi, jnp.where(at == 1, mid, jnp.where(at == 2, lo, 0.0))).astype(BF16)


def logs_of(message):
    block = message[STATE:, :].astype(F32)
    return jnp.sum(block[:8, :], axis=0, keepdims=True)


def state_of(message):
    return message[:STATE, :].astype(F32)


def prepare(log_ref, step_ref, imp_ref, b_ref, c_ref, gate_ref,
            w_ref, dt_ref, dtt_ref, q_ref, g_ref, bt_ref, tot_ref):
    lane = lax.broadcasted_iota(jnp.int32, (HERE, STRETCH), 1)
    cum = log_ref[...]
    shift = 1
    while shift < STRETCH:
        cum = cum + jnp.where(lane >= shift, pltpu.roll(cum, shift, 1), 0.0)
        shift *= 2
    step = step_ref[...] * imp_ref[...]
    tail = jnp.exp(cum[:, STRETCH - 1:] - cum)
    spread = (
        lax.broadcasted_iota(jnp.int32, (128, FEATS), 0) % HERE
        == lax.broadcasted_iota(jnp.int32, (128, FEATS), 1) // HEAD_DIM
    ).astype(F32).astype(BF16)
    blank = jnp.zeros((HERE, STRETCH), F32)

    def columns(v):
        hi, mid, lo = three_terms(v)
        return jnp.concatenate([hi, mid, lo, blank], axis=0).T.astype(BF16)

    def expand(v, into):
        for at in range(0, FEATS, 512):
            into(at, jnp.dot(v, spread[:, at:at + 512], preferred_element_type=F32))

    def put_dt(at, v):
        dt_ref[:, at:at + 512] = v

    def put_dtt(at, v):
        dtt_ref[:, at:at + 512] = v

    def put_gate(at, v):
        gate = gate_ref[:, at:at + 512].astype(F32)
        g = gate / (1.0 + jnp.exp(-gate))
        g_ref[:, at:at + 512] = g
        q_ref[:, at:at + 512] = v * g

    expand(columns(step), put_dt)
    expand(columns(step * tail), put_dtt)
    expand(columns(jnp.exp(cum)), put_gate)
    logs = columns(cum)
    last = jnp.broadcast_to(logs[STRETCH - 16:, :][15:, :], (16, 128))
    tot_ref[...] = jnp.dot(last, spread, preferred_element_type=F32)[:8]
    bt_ref[...] = b_ref[...].astype(F32).T.astype(BF16)

    scores = lax.dot_general(
        c_ref[...], b_ref[...], (((1,), (1,)), ((), ())), preferred_element_type=F32
    )
    cum_columns = jnp.concatenate([cum, blank, blank, blank], axis=0).T
    tri = (
        lax.broadcasted_iota(jnp.int32, (128, 128), 0)
        >= lax.broadcasted_iota(jnp.int32, (128, 128), 1)
    )
    for h in range(HERE):
        row = cum[h:h + 1, :]
        top = cum_columns[:128, h:h + 1]
        low = cum_columns[128:, h:h + 1]
        w_ref[h, :128, :128] = (
            jnp.exp(jnp.where(tri, top - row[:, :128], -1e30)) * scores[:128, :128]
        ).astype(BF16)
        w_ref[h, 128:, :128] = (jnp.exp(low - row[:, :128]) * scores[128:, :128]).astype(BF16)
        w_ref[h, 128:, 128:] = (
            jnp.exp(jnp.where(tri, low - row[:, 128:], -1e30)) * scores[128:, 128:]
        ).astype(BF16)


def end_state(x0, x1, x2, x3, dtt_ref, bt_ref, x_ref, keep_ref, send_ref, local):
    for k, piece in enumerate((x0, x1, x2, x3)):
        at = pl.multiple_of(place("head", -k, 4) * 64, 64)
        x_ref[pl.ds(at, 64), :] = piece[...]
    for at in range(0, FEATS, 256):
        decayed = (x_ref[:, at:at + 256].astype(F32) * dtt_ref[:, at:at + 256]).astype(BF16)
        local[:, at:at + 256] = jnp.dot(bt_ref[...], decayed, preferred_element_type=F32)
    core = lax.axis_index("core")
    keep_ref[...] = local[:, pl.ds(pl.multiple_of(core * HALF, HALF), HALF)]
    send_ref[...] = local[:, pl.ds(pl.multiple_of((1 - core) * HALF, HALF), HALF)].astype(BF16)


def inside(x_ref, dt_ref, w_ref, g_ref, skip_ref, p_ref):
    first = lax.broadcasted_iota(jnp.int32, (STRETCH, 128), 1) < HEAD_DIM
    for j in range(FEATS // 128):
        at = slice(j * 128, j * 128 + 128)
        x = x_ref[:, at].astype(F32)
        scaled = x * dt_ref[:, at]
        one = jnp.where(first, scaled, 0.0).astype(BF16)
        two = jnp.where(first, 0.0, scaled).astype(BF16)
        top = jnp.dot(w_ref[2 * j, :128, :128], one[:128], preferred_element_type=F32)
        top += jnp.dot(w_ref[2 * j + 1, :128, :128], two[:128], preferred_element_type=F32)
        low = jnp.dot(w_ref[2 * j, 128:, :], one, preferred_element_type=F32)
        low += jnp.dot(w_ref[2 * j + 1, 128:, :], two, preferred_element_type=F32)
        skip = skip_ref[:, at]
        p_ref[:128, at] = (top + skip * x[:128]) * g_ref[:128, at]
        p_ref[128:, at] = (low + skip * x[128:]) * g_ref[128:, at]


def halves(core, mine_ref, other_ref):
    at = pl.ds(pl.multiple_of(core * HALF, HALF), HALF)
    mine, other = mine_ref[:1, at], other_ref[:1, at]
    return pick(core, mine, other), pick(core, other, mine)


def chip_state(keep_ref, came_ref, tot_ref, tot_other_ref, s0, s1, s2, s3, message):
    core = lax.axis_index("core")
    log0, log1 = halves(core, tot_ref, tot_other_ref)
    keep, came = keep_ref[...], came_ref[...].astype(F32)
    message[:STATE, :] = (
        jnp.exp(log1) * pick(core, keep, came) + pick(core, came, keep)
    ).astype(BF16)
    message[STATE:, :] = log_block(log0 + log1)
    for k, out in enumerate((s0, s1, s2, s3)):
        out[...] = message[:, pl.ds(pl.multiple_of(place("x", k, 4) * PART, PART), PART)]


def row_state(m0, m1, m2, m3, all_ref, row_ref, state_ref):
    for k, piece in enumerate((m0, m1, m2, m3)):
        all_ref[place("x", -k, 4)] = piece[...]
    state = state_of(all_ref[0])
    logs = logs_of(all_ref[0])
    for x in range(1, 4):
        log = logs_of(all_ref[x])
        state = jnp.exp(log) * state + state_of(all_ref[x])
        logs = logs + log
    state_ref[...] = state
    row_ref[:STATE, :] = state.astype(BF16)
    row_ref[STATE:, :] = log_block(logs)


def window(row_ref, state_ref, before_ref, out_ref):
    z = lax.axis_index("z")
    log = logs_of(row_ref[...])
    before = state_of(before_ref[...])
    before = pick(jnp.minimum(z, 1), jnp.zeros_like(before), before)
    out_ref[:STATE, :] = (jnp.exp(log) * before + state_ref[...]).astype(BF16)
    out_ref[STATE:, :] = log_block(log + logs_of(before_ref[...]))


def enter(before_ref, p2, p4, p6, all_ref, e0, e1, e2, e3, every):
    z = lax.axis_index("z")
    state = jnp.zeros((STATE, PART), F32)
    for gap, piece in ((6, p6), (4, p4), (2, p2), (1, before_ref)):
        there = pick(lax.div(z, gap), jnp.zeros_like(state), state_of(piece[...]))
        state = jnp.exp(logs_of(piece[...])) * state + there
    for x in range(4):
        every[x] = state.astype(BF16)
        if x < 3:
            state = jnp.exp(logs_of(all_ref[x])) * state + state_of(all_ref[x])
    for k, out in enumerate((e0, e1, e2, e3)):
        out[...] = every[place("x", k, 4)]


def core_states(f0, f1, f2, f3, keep_ref, came_ref, tot_ref, tot_other_ref, own_ref, give_ref, chip):
    for k, piece in enumerate((f0, f1, f2, f3)):
        chip[:, pl.ds(pl.multiple_of(place("x", -k, 4) * PART, PART), PART)] = piece[...]
    core = lax.axis_index("core")
    log0, _ = halves(core, tot_ref, tot_other_ref)
    first = chip[...].astype(F32)
    local = pick(core, keep_ref[...], came_ref[...].astype(F32))
    second = jnp.exp(log0) * first + local
    own_ref[...] = pick(core, first, second).astype(BF16)
    give_ref[...] = pick(core, second, first).astype(BF16)


def gate_all(own_ref, came_ref, c_ref, p_ref, q_ref, gated_ref, sums_ref):
    core = lax.axis_index("core")
    total = jnp.zeros((STRETCH, 128), F32)
    for half in range(2):
        for at in range(0, HALF, 256):
            own, came = own_ref[:, at:at + 256].astype(F32), came_ref[:, at:at + 256].astype(F32)
            state = (pick(core, own, came) if half == 0 else pick(core, came, own)).astype(BF16)
            carried = jnp.dot(c_ref[...], state, preferred_element_type=F32)
            to = half * HALF + at
            gated = p_ref[:, to:to + 256] + q_ref[:, to:to + 256] * carried
            gated_ref[:, to:to + 256] = gated
            square = gated * gated
            total = total + square[:, :128] + square[:, 128:]
    sums_ref[...] = jnp.broadcast_to(jnp.sum(total.T, axis=0, keepdims=True), (8, STRETCH))


def normalize(gated_ref, q0, q1, q2, q3, gain_ref, out_ref):
    total = q0[:1, :] + q1[:1, :] + q2[:1, :] + q3[:1, :]
    scale = lax.rsqrt(total / (HEADS * HEAD_DIM) + epsilon)
    scale = jnp.broadcast_to(scale, (128, STRETCH)).T
    for at in range(0, FEATS, 128):
        out_ref[:, at:at + 128] = (
            gated_ref[:, at:at + 128] * scale * gain_ref[:, at:at + 128]
        ).astype(BF16)


def shifted(v, axis, step, size):
    return lax.ppermute(v, axis, [(i, (i + step) % size) for i in range(size)])


def on_device(inputs, gate, in_b, in_c, log_decay, step_size, importance, skip, norm_gain):
    y = lax.axis_index("head")
    pieces = [
        lax.dynamic_slice(inputs, (0, lax.rem(y + k, 4) * FEATS), (64, FEATS)) for k in range(4)
    ]
    pieces = [pieces[0]] + [shifted(pieces[k], "head", k, 4) for k in (1, 2, 3)]

    big = (STRETCH, FEATS)
    weights, dt, dtt, q, g, b_t, tot = kernel_call(
        prepare,
        [((HERE, STRETCH, STRETCH), BF16), (big, F32), (big, F32), (big, F32), (big, F32),
         ((STATE, STRETCH), BF16), ((8, FEATS), F32)],
        log_decay, step_size, importance.reshape(1, STRETCH), in_b, in_c, gate,
        flops=4 << 30, bytes_accessed=12 << 20,
    )
    tot_other = shifted(tot, "core", 1, 2)
    x, keep, send = kernel_call(
        end_state,
        [(big, BF16), ((STATE, HALF), F32), ((STATE, HALF), BF16)],
        *pieces, dtt, b_t,
        scratch=[((STATE, FEATS), F32)],
        flops=1 << 28, bytes_accessed=4 << 20,
    )
    came = shifted(send, "core", 1, 2)
    skip_row = jnp.repeat(skip, HEAD_DIM).reshape(1, FEATS)
    (p,) = kernel_call(
        inside, [(big, F32)], x, dt, weights, g, skip_row, flops=2 << 30, bytes_accessed=11 << 20
    )

    message = (STATE + LOGS, PART)
    slices = kernel_call(
        chip_state, [(message, BF16)] * 4, keep, came, tot, tot_other,
        scratch=[((STATE + LOGS, HALF), BF16)],
    )
    slices = [slices[0]] + [shifted(slices[k], "x", k, 4) for k in (1, 2, 3)]
    chips, row, state = kernel_call(
        row_state, [((4,) + message, BF16), (message, BF16), ((STATE, PART), F32)], *slices
    )
    before = shifted(row, "z", 1, 8)
    (pair,) = kernel_call(window, [(message, BF16)], row, state, before)
    back = [shifted(pair, "z", k, 8) for k in (2, 4, 6)]
    enters = kernel_call(
        enter, [((STATE, PART), BF16)] * 4, before, *back, chips,
        scratch=[((4, STATE, PART), BF16)],
    )
    enters = [enters[0]] + [shifted(enters[k], "x", k, 4) for k in (1, 2, 3)]
    own, give = kernel_call(
        core_states, [((STATE, HALF), BF16)] * 2, *enters, keep, came, tot, tot_other,
        scratch=[((STATE, HALF), BF16)],
    )
    got = shifted(give, "core", 1, 2)
    gated, sums = kernel_call(
        gate_all, [(big, F32), ((8, STRETCH), F32)], own, got, in_c, p, q
    )
    others = [shifted(sums, "head", k, 4) for k in (1, 2, 3)]
    (out,) = kernel_call(
        normalize, [(big, BF16)], gated, sums, *others, norm_gain.reshape(1, FEATS)
    )
    return out


def solution(mesh):
    fine = Mesh(mesh.devices.reshape(8, 4, 2, 4), ("z", "x", "core", "head"))
    seq = ("z", "x", "core")
    in_specs = (
        P(seq + ("head",), None),
        P(seq, "head"),
        P(seq, None),
        P(seq, None),
        P("head", seq),
        P("head", seq),
        P(seq),
        P("head"),
        P("head"),
    )
    return jax.shard_map(
        on_device, mesh=fine, in_specs=in_specs, out_specs=P(seq, "head"), check_vma=False
    )
```

```python
import functools

import jax
import jax.numpy as jnp
from jax import lax
from jax.experimental import pallas as pl
from jax.experimental.pallas import tpu as pltpu
from jax.sharding import Mesh, PartitionSpec as P

HEADS = 128
HEAD_DIM = 64
STATE = 128
STRETCH = 256
epsilon = 1e-05

F32 = jnp.float32
BF16 = jnp.bfloat16
HERE = 32
FEATS = HERE * HEAD_DIM
HALF = FEATS // 2
PART = HALF // 4
LOGS = 16


def kernel_call(body, outs, *args, scratch=(), after=(), flops=0, bytes_accessed=0):
    vmem = pl.BlockSpec(memory_space=pltpu.VMEM)
    count = len(args)

    def ordered(*refs):
        body(*refs[:count], *refs[count + len(after):])

    return pl.pallas_call(
        ordered,
        out_shape=[jax.ShapeDtypeStruct(s, d) for s, d in outs],
        in_specs=[vmem] * count + [pl.BlockSpec(memory_space=pl.ANY)] * len(after),
        out_specs=[vmem] * len(outs),
        scratch_shapes=[pltpu.VMEM(s, d) for s, d in scratch],
        compiler_params=pltpu.CompilerParams(vmem_limit_bytes=20 * 1024 * 1024),
        cost_estimate=pl.CostEstimate(
            flops=flops, bytes_accessed=bytes_accessed, transcendentals=0
        ),
    )(*args, *after)


def three_terms(v):
    hi = v.astype(BF16).astype(F32)
    rest = v - hi
    mid = rest.astype(BF16).astype(F32)
    return hi, mid, rest - mid


def pick(index, first, second):
    return jnp.where(jnp.full(first.shape, index, jnp.int32) == 0, first, second)


def place(axis, step, size):
    return lax.rem(lax.axis_index(axis) + (step + size), size)


def log_block(row):
    hi, mid, lo = three_terms(row)
    at = lax.broadcasted_iota(jnp.int32, (LOGS, row.shape[1]), 0)
    return jnp.where(at == 0, hi, jnp.where(at == 1, mid, jnp.where(at == 2, lo, 0.0))).astype(BF16)


def logs_of(message):
    block = message[STATE:, :].astype(F32)
    return jnp.sum(block[:8, :], axis=0, keepdims=True)


def state_of(message):
    return message[:STATE, :].astype(F32)


def cut(x_ref, s0, s1, s2, s3, sems):
    copies = []
    for k, out in enumerate((s0, s1, s2, s3)):
        at = pl.multiple_of(place("head", k, 4) * FEATS, FEATS)
        copies.append(pltpu.make_async_copy(x_ref.at[:, pl.ds(at, FEATS)], out, sems.at[k]))
    for copy in copies:
        copy.start()
    for copy in copies:
        copy.wait()


def prepare(log_ref, step_ref, imp_ref, b_ref, c_ref, gate_ref, skip_ref,
            w_ref, dt_ref, dtt_ref, q_ref, g_ref, bt_ref, tot_ref, skip_row_ref):
    lane = lax.broadcasted_iota(jnp.int32, (HERE, STRETCH), 1)
    cum = log_ref[...]
    shift = 1
    while shift < STRETCH:
        cum = cum + jnp.where(lane >= shift, pltpu.roll(cum, shift, 1), 0.0)
        shift *= 2
    step = step_ref[...] * imp_ref[...]
    tail = jnp.exp(cum[:, STRETCH - 1:] - cum)
    spread = (
        lax.broadcasted_iota(jnp.int32, (128, FEATS), 0) % HERE
        == lax.broadcasted_iota(jnp.int32, (128, FEATS), 1) // HEAD_DIM
    ).astype(F32).astype(BF16)
    blank = jnp.zeros((HERE, STRETCH), F32)

    def columns(v):
        hi, mid, lo = three_terms(v)
        return jnp.concatenate([hi, mid, lo, blank], axis=0).T.astype(BF16)

    def expand(v, into):
        for at in range(0, FEATS, 512):
            into(at, jnp.dot(v, spread[:, at:at + 512], preferred_element_type=F32))

    def put_dt(at, v):
        dt_ref[:, at:at + 512] = v

    def put_dtt(at, v):
        dtt_ref[:, at:at + 512] = v

    def put_gate(at, v):
        gate = gate_ref[:, at:at + 512].astype(F32)
        g = gate / (1.0 + jnp.exp(-gate))
        g_ref[:, at:at + 512] = g
        q_ref[:, at:at + 512] = v * g

    expand(columns(step), put_dt)
    expand(columns(step * tail), put_dtt)
    expand(columns(jnp.exp(cum)), put_gate)
    logs = columns(cum)
    last = jnp.broadcast_to(logs[STRETCH - 16:, :][15:, :], (16, 128))
    tot_ref[...] = jnp.dot(last, spread, preferred_element_type=F32)[:8]
    hi, mid, lo = three_terms(jnp.broadcast_to(skip_ref[...], (16, HERE)))
    skip = jnp.concatenate([hi, mid, lo, jnp.zeros_like(hi)], axis=1).astype(BF16)
    skip_row_ref[...] = jnp.dot(skip, spread, preferred_element_type=F32)[:8]
    bt_ref[...] = b_ref[...].astype(F32).T.astype(BF16)

    scores = lax.dot_general(
        c_ref[...], b_ref[...], (((1,), (1,)), ((), ())), preferred_element_type=F32
    )
    cum_columns = jnp.concatenate([cum, blank, blank, blank], axis=0).T
    tri = (
        lax.broadcasted_iota(jnp.int32, (128, 128), 0)
        >= lax.broadcasted_iota(jnp.int32, (128, 128), 1)
    )
    for h in range(HERE):
        row = cum[h:h + 1, :]
        top = cum_columns[:128, h:h + 1]
        low = cum_columns[128:, h:h + 1]
        w_ref[h, :128, :128] = (
            jnp.exp(jnp.where(tri, top - row[:, :128], -1e30)) * scores[:128, :128]
        ).astype(BF16)
        w_ref[h, 128:, :128] = (jnp.exp(low - row[:, :128]) * scores[128:, :128]).astype(BF16)
        w_ref[h, 128:, 128:] = (
            jnp.exp(jnp.where(tri, low - row[:, 128:], -1e30)) * scores[128:, 128:]
        ).astype(BF16)


def end_state(x0, x1, x2, x3, dtt_ref, bt_ref, x_ref, keep_ref, send_ref, local):
    for k, piece in enumerate((x0, x1, x2, x3)):
        at = pl.multiple_of(place("head", -k, 4) * 64, 64)
        x_ref[pl.ds(at, 64), :] = piece[...]
    for at in range(0, FEATS, 256):
        decayed = (x_ref[:, at:at + 256].astype(F32) * dtt_ref[:, at:at + 256]).astype(BF16)
        local[:, at:at + 256] = jnp.dot(bt_ref[...], decayed, preferred_element_type=F32)
    core = lax.axis_index("core")
    keep_ref[...] = local[:, pl.ds(pl.multiple_of(core * HALF, HALF), HALF)]
    send_ref[...] = local[:, pl.ds(pl.multiple_of((1 - core) * HALF, HALF), HALF)].astype(BF16)


def inside(x_ref, dt_ref, w_ref, g_ref, skip_ref, p_ref):
    first = lax.broadcasted_iota(jnp.int32, (STRETCH, 128), 1) < HEAD_DIM
    for j in range(FEATS // 128):
        at = slice(j * 128, j * 128 + 128)
        x = x_ref[:, at].astype(F32)
        scaled = x * dt_ref[:, at]
        one = jnp.where(first, scaled, 0.0).astype(BF16)
        two = jnp.where(first, 0.0, scaled).astype(BF16)
        top = jnp.dot(w_ref[2 * j, :128, :128], one[:128], preferred_element_type=F32)
        top += jnp.dot(w_ref[2 * j + 1, :128, :128], two[:128], preferred_element_type=F32)
        low = jnp.dot(w_ref[2 * j, 128:, :], one, preferred_element_type=F32)
        low += jnp.dot(w_ref[2 * j + 1, 128:, :], two, preferred_element_type=F32)
        skip = skip_ref[:1, at]
        p_ref[:128, at] = (top + skip * x[:128]) * g_ref[:128, at]
        p_ref[128:, at] = (low + skip * x[128:]) * g_ref[128:, at]


def halves(core, mine_ref, other_ref):
    at = pl.ds(pl.multiple_of(core * HALF, HALF), HALF)
    mine, other = mine_ref[:1, at], other_ref[:1, at]
    return pick(core, mine, other), pick(core, other, mine)


def chip_state(keep_ref, came_ref, tot_ref, tot_other_ref, s0, s1, s2, s3, message):
    core = lax.axis_index("core")
    log0, log1 = halves(core, tot_ref, tot_other_ref)
    keep, came = keep_ref[...], came_ref[...].astype(F32)
    message[:STATE, :] = (
        jnp.exp(log1) * pick(core, keep, came) + pick(core, came, keep)
    ).astype(BF16)
    message[STATE:, :] = log_block(log0 + log1)
    for k, out in enumerate((s0, s1, s2, s3)):
        out[...] = message[:, pl.ds(pl.multiple_of(place("x", k, 4) * PART, PART), PART)]


def row_state(m0, m1, m2, m3, all_ref, row_ref, state_ref):
    for k, piece in enumerate((m0, m1, m2, m3)):
        all_ref[place("x", -k, 4)] = piece[...]
    state = state_of(all_ref[0])
    logs = logs_of(all_ref[0])
    for x in range(1, 4):
        log = logs_of(all_ref[x])
        state = jnp.exp(log) * state + state_of(all_ref[x])
        logs = logs + log
    state_ref[...] = state
    row_ref[:STATE, :] = state.astype(BF16)
    row_ref[STATE:, :] = log_block(logs)


def window(row_ref, state_ref, before_ref, out_ref):
    z = lax.axis_index("z")
    log = logs_of(row_ref[...])
    before = state_of(before_ref[...])
    before = pick(jnp.minimum(z, 1), jnp.zeros_like(before), before)
    out_ref[:STATE, :] = (jnp.exp(log) * before + state_ref[...]).astype(BF16)
    out_ref[STATE:, :] = log_block(log + logs_of(before_ref[...]))


def enter(before_ref, p2, p4, p6, all_ref, e0, e1, e2, e3, every):
    z = lax.axis_index("z")
    state = jnp.zeros((STATE, PART), F32)
    for gap, piece in ((6, p6), (4, p4), (2, p2), (1, before_ref)):
        there = pick(lax.div(z, gap), jnp.zeros_like(state), state_of(piece[...]))
        state = jnp.exp(logs_of(piece[...])) * state + there
    for x in range(4):
        every[x] = state.astype(BF16)
        if x < 3:
            state = jnp.exp(logs_of(all_ref[x])) * state + state_of(all_ref[x])
    for k, out in enumerate((e0, e1, e2, e3)):
        out[...] = every[place("x", k, 4)]


def core_states(f0, f1, f2, f3, keep_ref, came_ref, tot_ref, tot_other_ref, own_ref, give_ref, chip):
    for k, piece in enumerate((f0, f1, f2, f3)):
        chip[:, pl.ds(pl.multiple_of(place("x", -k, 4) * PART, PART), PART)] = piece[...]
    core = lax.axis_index("core")
    log0, _ = halves(core, tot_ref, tot_other_ref)
    first = chip[...].astype(F32)
    local = pick(core, keep_ref[...], came_ref[...].astype(F32))
    second = jnp.exp(log0) * first + local
    own_ref[...] = pick(core, first, second).astype(BF16)
    give_ref[...] = pick(core, second, first).astype(BF16)


def gate_all(own_ref, came_ref, c_ref, p_ref, q_ref, gated_ref, sums_ref, states):
    core = lax.axis_index("core")
    states[:, pl.ds(pl.multiple_of(core * HALF, HALF), HALF)] = own_ref[...]
    states[:, pl.ds(pl.multiple_of((1 - core) * HALF, HALF), HALF)] = came_ref[...]
    total = jnp.zeros((STRETCH, 128), F32)
    for at in range(0, FEATS, 256):
        carried = jnp.dot(c_ref[...], states[:, at:at + 256], preferred_element_type=F32)
        gated = p_ref[:, at:at + 256] + q_ref[:, at:at + 256] * carried
        gated_ref[:, at:at + 256] = gated
        square = gated * gated
        total = total + square[:, :128] + square[:, 128:]
    sums_ref[...] = jnp.broadcast_to(jnp.sum(total.T, axis=0, keepdims=True), (8, STRETCH))


def normalize(gated_ref, q0, q1, q2, q3, gain_ref, out_ref):
    total = q0[:1, :] + q1[:1, :] + q2[:1, :] + q3[:1, :]
    scale = lax.rsqrt(total / (HEADS * HEAD_DIM) + epsilon)
    scale = jnp.broadcast_to(scale, (128, STRETCH)).T
    for at in range(0, FEATS, 128):
        out_ref[:, at:at + 128] = (
            gated_ref[:, at:at + 128] * scale * gain_ref[:, at:at + 128]
        ).astype(BF16)


def shifted(v, axis, step, size):
    return lax.ppermute(v, axis, [(i, (i + step) % size) for i in range(size)])


def on_device(inputs, gate, in_b, in_c, log_decay, step_size, importance, skip, norm_gain):
    pieces = pl.pallas_call(
        cut,
        out_shape=[jax.ShapeDtypeStruct((64, FEATS), BF16)] * 4,
        in_specs=[pl.BlockSpec(memory_space=pl.ANY)],
        out_specs=[pl.BlockSpec(memory_space=pltpu.VMEM)] * 4,
        scratch_shapes=[pltpu.SemaphoreType.DMA((4,))],
        compiler_params=pltpu.CompilerParams(vmem_limit_bytes=4 * 1024 * 1024),
    )(inputs)
    pieces = [pieces[0]] + [shifted(pieces[k], "head", k, 4) for k in (1, 2, 3)]

    big = (STRETCH, FEATS)
    weights, dt, dtt, q, g, b_t, tot, skip_row = kernel_call(
        prepare,
        [((HERE, STRETCH, STRETCH), BF16), (big, F32), (big, F32), (big, F32), (big, F32),
         ((STATE, STRETCH), BF16), ((8, FEATS), F32), ((8, FEATS), F32)],
        log_decay, step_size, importance.reshape(1, STRETCH), in_b, in_c, gate,
        skip.reshape(1, HERE),
        flops=4 << 30, bytes_accessed=12 << 20,
    )
    tot_other = shifted(tot, "core", 1, 2)
    x, keep, send = kernel_call(
        end_state,
        [(big, BF16), ((STATE, HALF), F32), ((STATE, HALF), BF16)],
        *pieces, dtt, b_t,
        scratch=[((STATE, FEATS), F32)],
        after=[tot_other],
        flops=1 << 28, bytes_accessed=4 << 20,
    )
    came = shifted(send, "core", 1, 2)
    (p,) = kernel_call(
        inside, [(big, F32)], x, dt, weights, g, skip_row, flops=2 << 30, bytes_accessed=11 << 20
    )

    message = (STATE + LOGS, PART)
    slices = kernel_call(
        chip_state, [(message, BF16)] * 4, keep, came, tot, tot_other,
        scratch=[((STATE + LOGS, HALF), BF16)],
        after=[p],
    )
    slices = [slices[0]] + [shifted(slices[k], "x", k, 4) for k in (1, 2, 3)]
    chips, row, state = kernel_call(
        row_state, [((4,) + message, BF16), (message, BF16), ((STATE, PART), F32)], *slices
    )
    before = shifted(row, "z", 1, 8)
    (pair,) = kernel_call(window, [(message, BF16)], row, state, before)
    back = [shifted(pair, "z", k, 8) for k in (2, 4, 6)]
    enters = kernel_call(
        enter, [((STATE, PART), BF16)] * 4, before, *back, chips,
        scratch=[((4, STATE, PART), BF16)],
    )
    enters = [enters[0]] + [shifted(enters[k], "x", k, 4) for k in (1, 2, 3)]
    own, give = kernel_call(
        core_states, [((STATE, HALF), BF16)] * 2, *enters, keep, came, tot, tot_other,
        scratch=[((STATE, HALF), BF16)],
    )
    got = shifted(give, "core", 1, 2)
    gated, sums = kernel_call(
        gate_all, [(big, F32), ((8, STRETCH), F32)], own, got, in_c, p, q,
        scratch=[((STATE, FEATS), BF16)],
    )
    others = [shifted(sums, "head", k, 4) for k in (1, 2, 3)]
    (out,) = kernel_call(
        normalize, [(big, BF16)], gated, sums, *others, norm_gain.reshape(1, FEATS)
    )
    return out


def solution(mesh):
    fine = Mesh(mesh.devices.reshape(8, 4, 2, 4), ("z", "x", "core", "head"))
    seq = ("z", "x", "core")
    in_specs = (
        P(seq + ("head",), None),
        P(seq, "head"),
        P(seq, None),
        P(seq, None),
        P("head", seq),
        P("head", seq),
        P(seq),
        P("head"),
        P("head"),
    )
    return jax.shard_map(
        on_device, mesh=fine, in_specs=in_specs, out_specs=P(seq, "head"), check_vma=False
    )
```

```python
import functools

import jax
import jax.numpy as jnp
from jax import lax
from jax.experimental import pallas as pl
from jax.experimental.pallas import tpu as pltpu
from jax.sharding import Mesh, PartitionSpec as P

HEADS = 128
HEAD_DIM = 64
STATE = 128
STRETCH = 256
epsilon = 1e-05

F32 = jnp.float32
BF16 = jnp.bfloat16
HERE = 32
FEATS = HERE * HEAD_DIM
HALF = FEATS // 2
PART = HALF // 4
STEPS = (0, 1, 3, 2)
LOGS = 16


def kernel_call(body, outs, *args, scratch=(), after=(), flops=0, bytes_accessed=0,
                hbm_in=False, hbm_out=False, copies=0):
    vmem, hbm = pl.BlockSpec(memory_space=pltpu.VMEM), pl.BlockSpec(memory_space=pltpu.HBM)
    count = len(args)

    def ordered(*refs):
        body(*refs[:count], *refs[count + len(after):])

    return pl.pallas_call(
        ordered,
        out_shape=[jax.ShapeDtypeStruct(s, d) for s, d in outs],
        in_specs=[hbm if hbm_in else vmem] * count
        + [pl.BlockSpec(memory_space=pl.ANY)] * len(after),
        out_specs=[hbm if hbm_out else vmem] * len(outs),
        scratch_shapes=[pltpu.VMEM(s, d) for s, d in scratch]
        + ([pltpu.SemaphoreType.DMA((copies,))] if copies else []),
        compiler_params=pltpu.CompilerParams(vmem_limit_bytes=20 * 1024 * 1024),
        cost_estimate=pl.CostEstimate(
            flops=flops, bytes_accessed=bytes_accessed, transcendentals=0
        ),
    )(*args, *after)


def three_terms(v):
    hi = v.astype(BF16).astype(F32)
    rest = v - hi
    mid = rest.astype(BF16).astype(F32)
    return hi, mid, rest - mid


def pick(index, first, second):
    return jnp.where(jnp.full(first.shape, index, jnp.int32) == 0, first, second)


def place(axis, step, size):
    return lax.rem(lax.axis_index(axis) + (step + size), size)


def log_block(row):
    hi, mid, lo = three_terms(row)
    at = lax.broadcasted_iota(jnp.int32, (LOGS, row.shape[1]), 0)
    return jnp.where(at == 0, hi, jnp.where(at == 1, mid, jnp.where(at == 2, lo, 0.0))).astype(BF16)


def logs_of(message):
    block = message[STATE:, :].astype(F32)
    return jnp.sum(block[:8, :], axis=0, keepdims=True)


def state_of(message):
    return message[:STATE, :].astype(F32)


def prepare(log_ref, step_ref, imp_ref, skip_ref, b_ref, c_ref, gate_ref,
            w_ref, dt_ref, dtt_ref, q_ref, g_ref, bt_ref, tot_ref, skip_row_ref):
    lane = lax.broadcasted_iota(jnp.int32, (HERE, STRETCH), 1)
    cum = log_ref[...]
    shift = 1
    while shift < STRETCH:
        cum = cum + jnp.where(lane >= shift, pltpu.roll(cum, shift, 1), 0.0)
        shift *= 2
    step = step_ref[...] * imp_ref[...]
    tail = jnp.exp(cum[:, STRETCH - 1:] - cum)
    spread = (
        lax.broadcasted_iota(jnp.int32, (128, FEATS), 0) % HERE
        == lax.broadcasted_iota(jnp.int32, (128, FEATS), 1) // HEAD_DIM
    ).astype(F32).astype(BF16)
    blank = jnp.zeros((HERE, STRETCH), F32)

    def columns(v):
        hi, mid, lo = three_terms(v)
        return jnp.concatenate([hi, mid, lo, blank], axis=0).T.astype(BF16)

    def expand(v, into):
        for at in range(0, FEATS, 512):
            into(at, jnp.dot(v, spread[:, at:at + 512], preferred_element_type=F32))

    def put_dt(at, v):
        dt_ref[:, at:at + 512] = v

    def put_dtt(at, v):
        dtt_ref[:, at:at + 512] = v

    def put_gate(at, v):
        gate = gate_ref[:, at:at + 512].astype(F32)
        g = gate / (1.0 + jnp.exp(-gate))
        g_ref[:, at:at + 512] = g
        q_ref[:, at:at + 512] = v * g

    expand(columns(step), put_dt)
    expand(columns(step * tail), put_dtt)
    expand(columns(jnp.exp(cum)), put_gate)
    logs = columns(cum)
    last = jnp.broadcast_to(logs[STRETCH - 16:, :][15:, :], (16, 128))
    tot_ref[...] = jnp.dot(last, spread, preferred_element_type=F32)[:8]
    hi, mid, lo = three_terms(jnp.broadcast_to(skip_ref[...], (16, HERE)))
    skip = jnp.concatenate([hi, mid, lo, jnp.zeros_like(hi)], axis=1).astype(BF16)
    skip_row_ref[...] = jnp.dot(skip, spread, preferred_element_type=F32)[:8]
    bt_ref[...] = b_ref[...].astype(F32).T.astype(BF16)

    scores = lax.dot_general(
        c_ref[...], b_ref[...], (((1,), (1,)), ((), ())), preferred_element_type=F32
    )
    cum_columns = jnp.concatenate([cum, blank, blank, blank], axis=0).T
    tri = (
        lax.broadcasted_iota(jnp.int32, (128, 128), 0)
        >= lax.broadcasted_iota(jnp.int32, (128, 128), 1)
    )
    for h in range(HERE):
        row = cum[h:h + 1, :]
        top = cum_columns[:128, h:h + 1]
        low = cum_columns[128:, h:h + 1]
        w_ref[h, :128, :128] = (
            jnp.exp(jnp.where(tri, top - row[:, :128], -1e30)) * scores[:128, :128]
        ).astype(BF16)
        w_ref[h, 128:, :128] = (jnp.exp(low - row[:, :128]) * scores[128:, :128]).astype(BF16)
        w_ref[h, 128:, 128:] = (
            jnp.exp(jnp.where(tri, low - row[:, 128:], -1e30)) * scores[128:, 128:]
        ).astype(BF16)


def end_state(x0, x1, x2, x3, dtt_ref, bt_ref, x_ref, keep_ref, send_ref, local):
    for k, piece in enumerate((x0, x1, x2, x3)):
        at = pl.multiple_of(place("head", -k, 4) * 64, 64)
        x_ref[pl.ds(at, 64), :] = piece[...]
    for at in range(0, FEATS, 256):
        decayed = (x_ref[:, at:at + 256].astype(F32) * dtt_ref[:, at:at + 256]).astype(BF16)
        local[:, at:at + 256] = jnp.dot(bt_ref[...], decayed, preferred_element_type=F32)
    core = lax.axis_index("core")
    keep_ref[...] = local[:, pl.ds(pl.multiple_of(core * HALF, HALF), HALF)]
    send_ref[...] = local[:, pl.ds(pl.multiple_of((1 - core) * HALF, HALF), HALF)].astype(BF16)


def inside(x_ref, dt_ref, w_ref, g_ref, skip_ref, p_ref):
    first = lax.broadcasted_iota(jnp.int32, (STRETCH, 128), 1) < HEAD_DIM
    for j in range(FEATS // 128):
        at = slice(j * 128, j * 128 + 128)
        x = x_ref[:, at].astype(F32)
        scaled = x * dt_ref[:, at]
        one = jnp.where(first, scaled, 0.0).astype(BF16)
        two = jnp.where(first, 0.0, scaled).astype(BF16)
        top = jnp.dot(w_ref[2 * j, :128, :128], one[:128], preferred_element_type=F32)
        top += jnp.dot(w_ref[2 * j + 1, :128, :128], two[:128], preferred_element_type=F32)
        low = jnp.dot(w_ref[2 * j, 128:, :], one, preferred_element_type=F32)
        low += jnp.dot(w_ref[2 * j + 1, 128:, :], two, preferred_element_type=F32)
        skip = skip_ref[:1, at]
        p_ref[:128, at] = (top + skip * x[:128]) * g_ref[:128, at]
        p_ref[128:, at] = (low + skip * x[128:]) * g_ref[128:, at]


def halves(core, mine_ref, other_ref):
    at = pl.ds(pl.multiple_of(core * HALF, HALF), HALF)
    mine, other = mine_ref[:1, at], other_ref[:1, at]
    return pick(core, mine, other), pick(core, other, mine)


def chip_state(keep_ref, came_ref, tot_ref, tot_other_ref, s0, s1, s2, s3, message):
    core = lax.axis_index("core")
    log0, log1 = halves(core, tot_ref, tot_other_ref)
    keep, came = keep_ref[...], came_ref[...].astype(F32)
    message[:STATE, :] = (
        jnp.exp(log1) * pick(core, keep, came) + pick(core, came, keep)
    ).astype(BF16)
    message[STATE:, :] = log_block(log0 + log1)
    for k, out in zip(STEPS, (s0, s1, s2, s3)):
        out[...] = message[:, pl.ds(pl.multiple_of(place("x", k, 4) * PART, PART), PART)]


def row_state(m0, m1, m2, m3, all_ref, row_ref, state_ref):
    for k, piece in zip(STEPS, (m0, m1, m2, m3)):
        all_ref[place("x", -k, 4)] = piece[...]
    state = state_of(all_ref[0])
    logs = logs_of(all_ref[0])
    for x in range(1, 4):
        log = logs_of(all_ref[x])
        state = jnp.exp(log) * state + state_of(all_ref[x])
        logs = logs + log
    state_ref[...] = state
    row_ref[:STATE, :] = state.astype(BF16)
    row_ref[STATE:, :] = log_block(logs)


def window(row_ref, state_ref, before_ref, after_ref, out_ref):
    z = lax.axis_index("z")
    log, log_after = logs_of(row_ref[...]), logs_of(after_ref[...])
    before = state_of(before_ref[...])
    before = pick(z, jnp.zeros_like(before), before)
    state = jnp.exp(log_after) * (jnp.exp(log) * before + state_ref[...])
    state = pick(7 - z, jnp.zeros_like(state), state) + state_of(after_ref[...])
    out_ref[:STATE, :] = state.astype(BF16)
    out_ref[STATE:, :] = log_block(log + log_after + logs_of(before_ref[...]))


def enter(before_ref, w3, w6, all_ref, e0, e1, e2, e3, every):
    z = lax.axis_index("z")
    state = jnp.zeros((STATE, PART), F32)
    for least, piece in ((5, w6), (2, w3), (1, before_ref)):
        there = pick(lax.div(z, least), jnp.zeros_like(state), state_of(piece[...]))
        state = jnp.exp(logs_of(piece[...])) * state + there
    for x in range(4):
        every[x] = state.astype(BF16)
        if x < 3:
            state = jnp.exp(logs_of(all_ref[x])) * state + state_of(all_ref[x])
    for k, out in zip(STEPS, (e0, e1, e2, e3)):
        out[...] = every[place("x", k, 4)]


def core_states(f0, f1, f2, f3, keep_ref, came_ref, tot_ref, tot_other_ref, own_ref, give_ref, chip):
    for k, piece in zip(STEPS, (f0, f1, f2, f3)):
        chip[:, pl.ds(pl.multiple_of(place("x", -k, 4) * PART, PART), PART)] = piece[...]
    core = lax.axis_index("core")
    log0, _ = halves(core, tot_ref, tot_other_ref)
    first = chip[...].astype(F32)
    local = pick(core, keep_ref[...], came_ref[...].astype(F32))
    second = jnp.exp(log0) * first + local
    own_ref[...] = pick(core, first, second).astype(BF16)
    give_ref[...] = pick(core, second, first).astype(BF16)


def gate_all(own_ref, came_ref, c_ref, p_ref, q_ref, gated_ref, sums_ref, states):
    core = lax.axis_index("core")
    states[:, pl.ds(pl.multiple_of(core * HALF, HALF), HALF)] = own_ref[...]
    states[:, pl.ds(pl.multiple_of((1 - core) * HALF, HALF), HALF)] = came_ref[...]
    total = jnp.zeros((STRETCH, 128), F32)
    for at in range(0, FEATS, 256):
        carried = jnp.dot(c_ref[...], states[:, at:at + 256], preferred_element_type=F32)
        gated = p_ref[:, at:at + 256] + q_ref[:, at:at + 256] * carried
        gated_ref[:, at:at + 256] = gated
        square = gated * gated
        total = total + square[:, :128] + square[:, 128:]
    sums_ref[...] = jnp.broadcast_to(jnp.sum(total.T, axis=0, keepdims=True), (8, STRETCH))


def normalize(gated_ref, q0, q1, q2, q3, gain_ref, out_hbm, out_ref, sems):
    total = q0[:1, :] + q1[:1, :] + q2[:1, :] + q3[:1, :]
    scale = lax.rsqrt(total / (HEADS * HEAD_DIM) + epsilon)
    scale = jnp.broadcast_to(scale, (128, STRETCH)).T
    copies = []
    for k in range(4):
        rows = slice(k * 64, k * 64 + 64)
        for at in range(0, FEATS, 128):
            out_ref[rows, at:at + 128] = (
                gated_ref[rows, at:at + 128] * scale[rows] * gain_ref[:, at:at + 128]
            ).astype(BF16)
        copy = pltpu.make_async_copy(out_ref.at[rows], out_hbm.at[rows], sems.at[k])
        copy.start()
        copies.append(copy)
    for copy in copies:
        copy.wait()


def shifted(v, axis, step, size):
    return lax.ppermute(v, axis, [(i, (i + step) % size) for i in range(size)])


def triple(pieces, axis, steps):
    return [shifted(piece, axis, k, 4) for k, piece in zip(steps, pieces[1:])]


def on_device(inputs, gate, in_b, in_c, log_decay, step_size, importance, skip, norm_gain):
    y = lax.axis_index("head")
    pieces = [
        lax.dynamic_slice(inputs, (0, lax.rem(y + k, 4) * FEATS), (64, FEATS)) for k in range(4)
    ]
    pieces = [pieces[0]] + triple(pieces, "head", (1, 2, 3))

    big = (STRETCH, FEATS)
    weights, dt, dtt, q, g, b_t, tot, skip_row = kernel_call(
        prepare,
        [((HERE, STRETCH, STRETCH), BF16), (big, F32), (big, F32), (big, F32), (big, F32),
         ((STATE, STRETCH), BF16), ((8, FEATS), F32), ((8, FEATS), F32)],
        log_decay, step_size, importance.reshape(1, STRETCH), skip.reshape(1, HERE),
        in_b, in_c, gate,
        flops=4 << 30, bytes_accessed=12 << 20,
    )
    tot_other = shifted(tot, "core", 1, 2)
    x, keep, send = kernel_call(
        end_state,
        [(big, BF16), ((STATE, HALF), F32), ((STATE, HALF), BF16)],
        *pieces, dtt, b_t,
        scratch=[((STATE, FEATS), F32)],
        after=[tot_other],
        flops=1 << 28, bytes_accessed=4 << 20,
    )
    came = shifted(send, "core", 1, 2)
    (p,) = kernel_call(
        inside, [(big, F32)], x, dt, weights, g, skip_row, flops=2 << 30, bytes_accessed=11 << 20
    )

    message = (STATE + LOGS, PART)
    slices = kernel_call(
        chip_state, [(message, BF16)] * 4, keep, came, tot, tot_other,
        scratch=[((STATE + LOGS, HALF), BF16)],
        after=[p],
    )
    slices = [slices[0]] + triple(slices, "x", STEPS[1:])
    chips, row, state = kernel_call(
        row_state, [((4,) + message, BF16), (message, BF16), ((STATE, PART), F32)], *slices
    )
    before = shifted(row, "z", 1, 8)
    after = shifted(row, "z", 7, 8)
    (three,) = kernel_call(window, [(message, BF16)], row, state, before, after)
    back = [shifted(three, "z", 3, 8), shifted(three, "z", 6, 8)]
    enters = kernel_call(
        enter, [((STATE, PART), BF16)] * 4, before, *back, chips,
        scratch=[((4, STATE, PART), BF16)],
    )
    enters = [enters[0]] + triple(enters, "x", STEPS[1:])
    own, give = kernel_call(
        core_states, [((STATE, HALF), BF16)] * 2, *enters, keep, came, tot, tot_other,
        scratch=[((STATE, HALF), BF16)],
    )
    got = shifted(give, "core", 1, 2)
    gated, sums = kernel_call(
        gate_all, [(big, F32), ((8, STRETCH), F32)], own, got, in_c, p, q,
        scratch=[((STATE, FEATS), BF16)],
    )
    others = triple([sums] * 4, "head", (2, 3, 1))
    (out,) = kernel_call(
        normalize, [(big, BF16)], gated, sums, *others, norm_gain.reshape(1, FEATS),
        scratch=[(big, BF16)], hbm_out=True, copies=4,
    )
    return out


def solution(mesh):
    fine = Mesh(mesh.devices.reshape(8, 4, 2, 4), ("z", "x", "core", "head"))
    seq = ("z", "x", "core")
    in_specs = (
        P(seq + ("head",), None),
        P(seq, "head"),
        P(seq, None),
        P(seq, None),
        P("head", seq),
        P("head", seq),
        P(seq),
        P("head"),
        P("head"),
    )
    return jax.shard_map(
        on_device, mesh=fine, in_specs=in_specs, out_specs=P(seq, "head"), check_vma=False
    )
```

```python
import functools

import jax
import jax.numpy as jnp
from jax import lax
from jax.experimental import pallas as pl
from jax.experimental.pallas import tpu as pltpu
from jax.sharding import Mesh, PartitionSpec as P

HEADS = 128
HEAD_DIM = 64
STATE = 128
STRETCH = 256
epsilon = 1e-05

F32 = jnp.float32
BF16 = jnp.bfloat16
HERE = 32
FEATS = HERE * HEAD_DIM
HALF = FEATS // 2
PART = HALF // 4
ROUND_Y = (0, 2, 3, 1)
ROUND_X = (0, 1, 2, 3)
LOGS = 16


def kernel_call(body, outs, *args, scratch=(), after=(), flops=0, bytes_accessed=0,
                hbm_in=False, hbm_out=False, copies=0):
    vmem, hbm = pl.BlockSpec(memory_space=pltpu.VMEM), pl.BlockSpec(memory_space=pltpu.HBM)
    count = len(args)

    def ordered(*refs):
        body(*refs[:count], *refs[count + len(after):])

    return pl.pallas_call(
        ordered,
        out_shape=[jax.ShapeDtypeStruct(s, d) for s, d in outs],
        in_specs=[hbm if hbm_in else vmem] * count
        + [pl.BlockSpec(memory_space=pl.ANY)] * len(after),
        out_specs=[hbm if hbm_out else vmem] * len(outs),
        scratch_shapes=[pltpu.VMEM(s, d) for s, d in scratch]
        + ([pltpu.SemaphoreType.DMA((copies,))] if copies else []),
        compiler_params=pltpu.CompilerParams(vmem_limit_bytes=20 * 1024 * 1024),
        cost_estimate=pl.CostEstimate(
            flops=flops, bytes_accessed=bytes_accessed, transcendentals=0
        ),
    )(*args, *after)


def three_terms(v):
    hi = v.astype(BF16).astype(F32)
    rest = v - hi
    mid = rest.astype(BF16).astype(F32)
    return hi, mid, rest - mid


def pick(index, first, second):
    return jnp.where(jnp.full(first.shape, index, jnp.int32) == 0, first, second)


def place(axis, step, size):
    return lax.rem(lax.axis_index(axis) + (step + size), size)


def log_block(row):
    hi, mid, lo = three_terms(row)
    at = lax.broadcasted_iota(jnp.int32, (LOGS, row.shape[1]), 0)
    return jnp.where(at == 0, hi, jnp.where(at == 1, mid, jnp.where(at == 2, lo, 0.0))).astype(BF16)


def logs_of(message):
    block = message[STATE:, :].astype(F32)
    return jnp.sum(block[:8, :], axis=0, keepdims=True)


def state_of(message):
    return message[:STATE, :].astype(F32)


def prepare(log_ref, step_ref, imp_ref, skip_ref, b_ref, c_ref, gate_ref,
            w_ref, dt_ref, dtt_ref, q_ref, g_ref, bt_ref, tot_ref, skip_row_ref):
    lane = lax.broadcasted_iota(jnp.int32, (HERE, STRETCH), 1)
    cum = log_ref[...]
    shift = 1
    while shift < STRETCH:
        cum = cum + jnp.where(lane >= shift, pltpu.roll(cum, shift, 1), 0.0)
        shift *= 2
    step = step_ref[...] * imp_ref[...]
    tail = jnp.exp(cum[:, STRETCH - 1:] - cum)
    spread = (
        lax.broadcasted_iota(jnp.int32, (128, FEATS), 0) % HERE
        == lax.broadcasted_iota(jnp.int32, (128, FEATS), 1) // HEAD_DIM
    ).astype(F32).astype(BF16)
    blank = jnp.zeros((HERE, STRETCH), F32)

    def columns(v):
        hi, mid, lo = three_terms(v)
        return jnp.concatenate([hi, mid, lo, blank], axis=0).T.astype(BF16)

    def expand(v, into):
        for at in range(0, FEATS, 512):
            into(at, jnp.dot(v, spread[:, at:at + 512], preferred_element_type=F32))

    def put_dt(at, v):
        dt_ref[:, at:at + 512] = v

    def put_dtt(at, v):
        dtt_ref[:, at:at + 512] = v

    def put_gate(at, v):
        gate = gate_ref[:, at:at + 512].astype(F32)
        g = gate / (1.0 + jnp.exp(-gate))
        g_ref[:, at:at + 512] = g
        q_ref[:, at:at + 512] = v * g

    expand(columns(step), put_dt)
    expand(columns(step * tail), put_dtt)
    expand(columns(jnp.exp(cum)), put_gate)
    logs = columns(cum)
    last = jnp.broadcast_to(logs[STRETCH - 16:, :][15:, :], (16, 128))
    tot_ref[...] = jnp.dot(last, spread, preferred_element_type=F32)[:8]
    hi, mid, lo = three_terms(jnp.broadcast_to(skip_ref[...], (16, HERE)))
    skip = jnp.concatenate([hi, mid, lo, jnp.zeros_like(hi)], axis=1).astype(BF16)
    skip_row_ref[...] = jnp.dot(skip, spread, preferred_element_type=F32)[:8]
    bt_ref[...] = b_ref[...].astype(F32).T.astype(BF16)

    scores = lax.dot_general(
        c_ref[...], b_ref[...], (((1,), (1,)), ((), ())), preferred_element_type=F32
    )
    cum_columns = jnp.concatenate([cum, blank, blank, blank], axis=0).T
    tri = (
        lax.broadcasted_iota(jnp.int32, (128, 128), 0)
        >= lax.broadcasted_iota(jnp.int32, (128, 128), 1)
    )
    for h in range(HERE):
        row = cum[h:h + 1, :]
        top = cum_columns[:128, h:h + 1]
        low = cum_columns[128:, h:h + 1]
        w_ref[h, :128, :128] = (
            jnp.exp(jnp.where(tri, top - row[:, :128], -1e30)) * scores[:128, :128]
        ).astype(BF16)
        w_ref[h, 128:, :128] = (jnp.exp(low - row[:, :128]) * scores[128:, :128]).astype(BF16)
        w_ref[h, 128:, 128:] = (
            jnp.exp(jnp.where(tri, low - row[:, 128:], -1e30)) * scores[128:, 128:]
        ).astype(BF16)


def end_state(x0, x1, x2, x3, dtt_ref, bt_ref, x_ref, keep_ref, send_ref, local):
    for k, piece in zip(ROUND_Y, (x0, x1, x2, x3)):
        at = pl.multiple_of(place("head", -k, 4) * 64, 64)
        x_ref[pl.ds(at, 64), :] = piece[...]
    for at in range(0, FEATS, 256):
        decayed = (x_ref[:, at:at + 256].astype(F32) * dtt_ref[:, at:at + 256]).astype(BF16)
        local[:, at:at + 256] = jnp.dot(bt_ref[...], decayed, preferred_element_type=F32)
    core = lax.axis_index("core")
    keep_ref[...] = local[:, pl.ds(pl.multiple_of(core * HALF, HALF), HALF)]
    send_ref[...] = local[:, pl.ds(pl.multiple_of((1 - core) * HALF, HALF), HALF)].astype(BF16)


def inside(x_ref, dt_ref, w_ref, g_ref, skip_ref, p_ref):
    first = lax.broadcasted_iota(jnp.int32, (STRETCH, 128), 1) < HEAD_DIM
    for j in range(FEATS // 128):
        at = slice(j * 128, j * 128 + 128)
        x = x_ref[:, at].astype(F32)
        scaled = x * dt_ref[:, at]
        one = jnp.where(first, scaled, 0.0).astype(BF16)
        two = jnp.where(first, 0.0, scaled).astype(BF16)
        top = jnp.dot(w_ref[2 * j, :128, :128], one[:128], preferred_element_type=F32)
        top += jnp.dot(w_ref[2 * j + 1, :128, :128], two[:128], preferred_element_type=F32)
        low = jnp.dot(w_ref[2 * j, 128:, :], one, preferred_element_type=F32)
        low += jnp.dot(w_ref[2 * j + 1, 128:, :], two, preferred_element_type=F32)
        skip = skip_ref[:1, at]
        p_ref[:128, at] = (top + skip * x[:128]) * g_ref[:128, at]
        p_ref[128:, at] = (low + skip * x[128:]) * g_ref[128:, at]


def halves(core, mine_ref, other_ref):
    at = pl.ds(pl.multiple_of(core * HALF, HALF), HALF)
    mine, other = mine_ref[:1, at], other_ref[:1, at]
    return pick(core, mine, other), pick(core, other, mine)


def chip_state(keep_ref, came_ref, tot_ref, tot_other_ref, s0, s1, s2, s3, message):
    core = lax.axis_index("core")
    log0, log1 = halves(core, tot_ref, tot_other_ref)
    keep, came = keep_ref[...], came_ref[...].astype(F32)
    message[:STATE, :] = (
        jnp.exp(log1) * pick(core, keep, came) + pick(core, came, keep)
    ).astype(BF16)
    message[STATE:, :] = log_block(log0 + log1)
    for k, out in zip(ROUND_X, (s0, s1, s2, s3)):
        out[...] = message[:, pl.ds(pl.multiple_of(place("x", k, 4) * PART, PART), PART)]


def row_state(m0, m1, m2, m3, all_ref, row_ref):
    for k, piece in zip(ROUND_X, (m0, m1, m2, m3)):
        all_ref[place("x", -k, 4)] = piece[...]
    state = state_of(all_ref[0])
    logs = logs_of(all_ref[0])
    for x in range(1, 4):
        log = logs_of(all_ref[x])
        state = jnp.exp(log) * state + state_of(all_ref[x])
        logs = logs + log
    row_ref[:STATE, :] = state.astype(BF16)
    row_ref[STATE:, :] = log_block(logs)


def four_rows(r0, r1, r2, r3, inner_ref, logs_ref, total_ref, rows):
    for k, piece in enumerate((r0, r1, r2, r3)):
        rows[lax.rem(lax.axis_index("z") + 4 - k, 4)] = piece[...]
    me = lax.rem(lax.axis_index("z"), 4)
    state, logs = state_of(rows[0]), logs_of(rows[0])
    inner, before = jnp.zeros_like(state), jnp.zeros_like(logs)
    for z in range(1, 4):
        inner, before = pick(me - z, state, inner), pick(me - z, logs, before)
        log = logs_of(rows[z])
        state = jnp.exp(log) * state + state_of(rows[z])
        logs = logs + log
    inner_ref[...] = inner
    logs_ref[...] = jnp.broadcast_to(before, (8, PART))
    total_ref[...] = state.astype(BF16)


def enter(inner_ref, logs_ref, far_ref, all_ref, e0, e1, e2, e3, every):
    state = jnp.exp(logs_ref[:1, :]) * pick(lax.div(lax.axis_index("z"), 4), jnp.zeros((STATE, PART), F32), far_ref[...].astype(F32)) + inner_ref[...]
    for x in range(4):
        every[x] = state.astype(BF16)
        if x < 3:
            state = jnp.exp(logs_of(all_ref[x])) * state + state_of(all_ref[x])
    for k, out in zip(ROUND_X, (e0, e1, e2, e3)):
        out[...] = every[place("x", k, 4)]


def core_states(f0, f1, f2, f3, keep_ref, came_ref, tot_ref, tot_other_ref, own_ref, give_ref, chip):
    for k, piece in zip(ROUND_X, (f0, f1, f2, f3)):
        chip[:, pl.ds(pl.multiple_of(place("x", -k, 4) * PART, PART), PART)] = piece[...]
    core = lax.axis_index("core")
    log0, _ = halves(core, tot_ref, tot_other_ref)
    first = chip[...].astype(F32)
    local = pick(core, keep_ref[...], came_ref[...].astype(F32))
    second = jnp.exp(log0) * first + local
    own_ref[...] = pick(core, first, second).astype(BF16)
    give_ref[...] = pick(core, second, first).astype(BF16)


def gate_all(own_ref, came_ref, c_ref, p_ref, q_ref, gated_ref, sums_ref, states):
    core = lax.axis_index("core")
    states[:, pl.ds(pl.multiple_of(core * HALF, HALF), HALF)] = own_ref[...]
    states[:, pl.ds(pl.multiple_of((1 - core) * HALF, HALF), HALF)] = came_ref[...]
    total = jnp.zeros((STRETCH, 128), F32)
    for at in range(0, FEATS, 256):
        carried = jnp.dot(c_ref[...], states[:, at:at + 256], preferred_element_type=F32)
        gated = p_ref[:, at:at + 256] + q_ref[:, at:at + 256] * carried
        gated_ref[:, at:at + 256] = gated
        square = gated * gated
        total = total + square[:, :128] + square[:, 128:]
    sums_ref[...] = jnp.broadcast_to(jnp.sum(total.T, axis=0, keepdims=True), (8, STRETCH))


def normalize(gated_ref, q0, q1, q2, q3, gain_ref, out_hbm, out_ref, sems):
    total = q0[:1, :] + q1[:1, :] + q2[:1, :] + q3[:1, :]
    scale = lax.rsqrt(total / (HEADS * HEAD_DIM) + epsilon)
    scale = jnp.broadcast_to(scale, (128, STRETCH)).T
    copies = []
    for k in range(4):
        rows = slice(k * 64, k * 64 + 64)
        for at in range(0, FEATS, 128):
            out_ref[rows, at:at + 128] = (
                gated_ref[rows, at:at + 128] * scale[rows] * gain_ref[:, at:at + 128]
            ).astype(BF16)
        copy = pltpu.make_async_copy(out_ref.at[rows], out_hbm.at[rows], sems.at[k])
        copy.start()
        copies.append(copy)
    for copy in copies:
        copy.wait()


def shifted(v, axis, step, size):
    return lax.ppermute(v, axis, [(i, (i + step) % size) for i in range(size)])


def triple(pieces, axis, steps):
    return [shifted(piece, axis, k, 4) for k, piece in zip(steps, pieces[1:])]


def on_device(inputs, gate, in_b, in_c, log_decay, step_size, importance, skip, norm_gain):
    y = lax.axis_index("head")
    pieces = [
        lax.dynamic_slice(inputs, (0, lax.rem(y + k, 4) * FEATS), (64, FEATS)) for k in ROUND_Y
    ]
    pieces = [pieces[0]] + triple(pieces, "head", ROUND_Y[1:])

    big = (STRETCH, FEATS)
    weights, dt, dtt, q, g, b_t, tot, skip_row = kernel_call(
        prepare,
        [((HERE, STRETCH, STRETCH), BF16), (big, F32), (big, F32), (big, F32), (big, F32),
         ((STATE, STRETCH), BF16), ((8, FEATS), F32), ((8, FEATS), F32)],
        log_decay, step_size, importance.reshape(1, STRETCH), skip.reshape(1, HERE),
        in_b, in_c, gate,
        flops=4 << 30, bytes_accessed=12 << 20,
    )
    tot_other = shifted(tot, "core", 1, 2)
    x, keep, send = kernel_call(
        end_state,
        [(big, BF16), ((STATE, HALF), F32), ((STATE, HALF), BF16)],
        *pieces, dtt, b_t,
        scratch=[((STATE, FEATS), F32)],
        after=[tot_other],
        flops=1 << 28, bytes_accessed=4 << 20,
    )
    came = shifted(send, "core", 1, 2)
    (p,) = kernel_call(
        inside, [(big, F32)], x, dt, weights, g, skip_row, flops=2 << 30, bytes_accessed=11 << 20
    )

    message = (STATE + LOGS, PART)
    slices = kernel_call(
        chip_state, [(message, BF16)] * 4, keep, came, tot, tot_other,
        scratch=[((STATE + LOGS, HALF), BF16)],
        after=[p],
    )
    slices = [slices[0]] + triple(slices, "x", ROUND_X[1:])
    chips, row = kernel_call(
        row_state, [((4,) + message, BF16), (message, BF16)], *slices
    )
    near = [
        lax.ppermute(row, "z", [(i, i // 4 * 4 + (i + k) % 4) for i in range(8)]) for k in (1, 2, 3)
    ]
    inner, logs, total = kernel_call(
        four_rows, [((STATE, PART), F32), ((8, PART), F32), ((STATE, PART), BF16)], row, *near,
        scratch=[((4,) + message, BF16)],
    )
    far = lax.ppermute(total, "z", [(i, 7 - i) for i in range(8)])
    enters = kernel_call(
        enter, [((STATE, PART), BF16)] * 4, inner, logs, far, chips,
        scratch=[((4, STATE, PART), BF16)],
    )
    enters = [enters[0]] + triple(enters, "x", ROUND_X[1:])
    own, give = kernel_call(
        core_states, [((STATE, HALF), BF16)] * 2, *enters, keep, came, tot, tot_other,
        scratch=[((STATE, HALF), BF16)],
    )
    got = shifted(give, "core", 1, 2)
    gated, sums = kernel_call(
        gate_all, [(big, F32), ((8, STRETCH), F32)], own, got, in_c, p, q,
        scratch=[((STATE, FEATS), BF16)],
    )
    others = triple([sums] * 4, "head", (1, 2, 3))
    (out,) = kernel_call(
        normalize, [(big, BF16)], gated, sums, *others, norm_gain.reshape(1, FEATS),
        scratch=[(big, BF16)], hbm_out=True, copies=4,
    )
    return out


def solution(mesh):
    fine = Mesh(mesh.devices.reshape(8, 4, 2, 4), ("z", "x", "core", "head"))
    seq = ("z", "x", "core")
    in_specs = (
        P(seq + ("head",), None),
        P(seq, "head"),
        P(seq, None),
        P(seq, None),
        P("head", seq),
        P("head", seq),
        P(seq),
        P("head"),
        P("head"),
    )
    return jax.shard_map(
        on_device, mesh=fine, in_specs=in_specs, out_specs=P(seq, "head"), check_vma=False
    )
```

```python
import functools

import jax
import jax.numpy as jnp
from jax import lax
from jax.experimental import pallas as pl
from jax.experimental.pallas import tpu as pltpu
from jax.sharding import Mesh, PartitionSpec as P

HEADS = 128
HEAD_DIM = 64
STATE = 128
STRETCH = 256
epsilon = 1e-05

F32 = jnp.float32
BF16 = jnp.bfloat16
HERE = 32
FEATS = HERE * HEAD_DIM
HALF = FEATS // 2
PART = HALF // 4
ROUND_Y = (0, 2, 3, 1)
ROUND_X = (0, 1, 2, 3)
LOGS = 16


def kernel_call(body, outs, *args, scratch=(), after=(), flops=0, bytes_accessed=0,
                hbm_in=False, hbm_out=False, copies=0):
    vmem, hbm = pl.BlockSpec(memory_space=pltpu.VMEM), pl.BlockSpec(memory_space=pltpu.HBM)
    count = len(args)

    def ordered(*refs):
        body(*refs[:count], *refs[count + len(after):])

    return pl.pallas_call(
        ordered,
        out_shape=[jax.ShapeDtypeStruct(s, d) for s, d in outs],
        in_specs=[hbm if hbm_in else vmem] * count
        + [pl.BlockSpec(memory_space=pl.ANY)] * len(after),
        out_specs=[hbm if hbm_out else vmem] * len(outs),
        scratch_shapes=[pltpu.VMEM(s, d) for s, d in scratch]
        + ([pltpu.SemaphoreType.DMA((copies,))] if copies else []),
        compiler_params=pltpu.CompilerParams(vmem_limit_bytes=20 * 1024 * 1024),
        cost_estimate=pl.CostEstimate(
            flops=flops, bytes_accessed=bytes_accessed, transcendentals=0
        ),
    )(*args, *after)


def three_terms(v):
    hi = v.astype(BF16).astype(F32)
    rest = v - hi
    mid = rest.astype(BF16).astype(F32)
    return hi, mid, rest - mid


def pick(index, first, second):
    return jnp.where(jnp.full(first.shape, index, jnp.int32) == 0, first, second)


def place(axis, step, size):
    return lax.rem(lax.axis_index(axis) + (step + size), size)


def log_block(row):
    hi, mid, lo = three_terms(row)
    at = lax.broadcasted_iota(jnp.int32, (LOGS, row.shape[1]), 0)
    return jnp.where(at == 0, hi, jnp.where(at == 1, mid, jnp.where(at == 2, lo, 0.0))).astype(BF16)


def logs_of(message):
    block = message[STATE:, :].astype(F32)
    return jnp.sum(block[:8, :], axis=0, keepdims=True)


def state_of(message):
    return message[:STATE, :].astype(F32)


def prepare(log_ref, step_ref, imp_ref, skip_ref, b_ref, c_ref, gate_ref,
            w_ref, dt_ref, dtt_ref, q_ref, g_ref, bt_ref, tot_ref, skip_row_ref):
    lane = lax.broadcasted_iota(jnp.int32, (HERE, STRETCH), 1)
    cum = log_ref[...]
    shift = 1
    while shift < STRETCH:
        cum = cum + jnp.where(lane >= shift, pltpu.roll(cum, shift, 1), 0.0)
        shift *= 2
    step = step_ref[...] * imp_ref[...]
    tail = jnp.exp(cum[:, STRETCH - 1:] - cum)
    spread = (
        lax.broadcasted_iota(jnp.int32, (128, FEATS), 0) % HERE
        == lax.broadcasted_iota(jnp.int32, (128, FEATS), 1) // HEAD_DIM
    ).astype(F32).astype(BF16)
    blank = jnp.zeros((HERE, STRETCH), F32)

    def columns(v):
        hi, mid, lo = three_terms(v)
        return jnp.concatenate([hi, mid, lo, blank], axis=0).T.astype(BF16)

    def expand(v, into):
        for at in range(0, FEATS, 512):
            into(at, jnp.dot(v, spread[:, at:at + 512], preferred_element_type=F32))

    def put_dt(at, v):
        dt_ref[:, at:at + 512] = v

    def put_dtt(at, v):
        dtt_ref[:, at:at + 512] = v

    def put_gate(at, v):
        gate = gate_ref[:, at:at + 512].astype(F32)
        g = gate / (1.0 + jnp.exp(-gate))
        g_ref[:, at:at + 512] = g
        q_ref[:, at:at + 512] = v * g

    expand(columns(step), put_dt)
    expand(columns(step * tail), put_dtt)
    expand(columns(jnp.exp(cum)), put_gate)
    logs = columns(cum)
    last = jnp.broadcast_to(logs[STRETCH - 16:, :][15:, :], (16, 128))
    tot_ref[...] = jnp.dot(last, spread, preferred_element_type=F32)[:8]
    hi, mid, lo = three_terms(jnp.broadcast_to(skip_ref[...], (16, HERE)))
    skip = jnp.concatenate([hi, mid, lo, jnp.zeros_like(hi)], axis=1).astype(BF16)
    skip_row_ref[...] = jnp.dot(skip, spread, preferred_element_type=F32)[:8]
    bt_ref[...] = b_ref[...].astype(F32).T.astype(BF16)

    scores = lax.dot_general(
        c_ref[...], b_ref[...], (((1,), (1,)), ((), ())), preferred_element_type=F32
    )
    cum_columns = jnp.concatenate([cum, blank, blank, blank], axis=0).T
    tri = (
        lax.broadcasted_iota(jnp.int32, (128, 128), 0)
        >= lax.broadcasted_iota(jnp.int32, (128, 128), 1)
    )
    for h in range(HERE):
        row = cum[h:h + 1, :]
        top = cum_columns[:128, h:h + 1]
        low = cum_columns[128:, h:h + 1]
        w_ref[h, :128, :128] = (
            jnp.exp(jnp.where(tri, top - row[:, :128], -1e30)) * scores[:128, :128]
        ).astype(BF16)
        w_ref[h, 128:, :128] = (jnp.exp(low - row[:, :128]) * scores[128:, :128]).astype(BF16)
        w_ref[h, 128:, 128:] = (
            jnp.exp(jnp.where(tri, low - row[:, 128:], -1e30)) * scores[128:, 128:]
        ).astype(BF16)


def end_state(all_ref, x1, x2, x3, dtt_ref, bt_ref, x_ref, keep_ref, send_ref, local):
    y = lax.axis_index("head")
    own = pl.ds(pl.multiple_of(y * FEATS, FEATS), FEATS)
    x_ref[pl.ds(pl.multiple_of(y * 64, 64), 64), :] = all_ref[:, own]
    for k, piece in zip(ROUND_Y[1:], (x1, x2, x3)):
        at = pl.multiple_of(place("head", -k, 4) * 64, 64)
        x_ref[pl.ds(at, 64), :] = piece[...]
    for at in range(0, FEATS, 256):
        decayed = (x_ref[:, at:at + 256].astype(F32) * dtt_ref[:, at:at + 256]).astype(BF16)
        local[:, at:at + 256] = jnp.dot(bt_ref[...], decayed, preferred_element_type=F32)
    core = lax.axis_index("core")
    keep_ref[...] = local[:, pl.ds(pl.multiple_of(core * HALF, HALF), HALF)]
    send_ref[...] = local[:, pl.ds(pl.multiple_of((1 - core) * HALF, HALF), HALF)].astype(BF16)


def inside(x_ref, dt_ref, w_ref, g_ref, skip_ref, p_ref):
    first = lax.broadcasted_iota(jnp.int32, (STRETCH, 128), 1) < HEAD_DIM
    for j in range(FEATS // 128):
        at = slice(j * 128, j * 128 + 128)
        x = x_ref[:, at].astype(F32)
        scaled = x * dt_ref[:, at]
        one = jnp.where(first, scaled, 0.0).astype(BF16)
        two = jnp.where(first, 0.0, scaled).astype(BF16)
        top = jnp.dot(w_ref[2 * j, :128, :128], one[:128], preferred_element_type=F32)
        top += jnp.dot(w_ref[2 * j + 1, :128, :128], two[:128], preferred_element_type=F32)
        low = jnp.dot(w_ref[2 * j, 128:, :], one, preferred_element_type=F32)
        low += jnp.dot(w_ref[2 * j + 1, 128:, :], two, preferred_element_type=F32)
        skip = skip_ref[:1, at]
        p_ref[:128, at] = (top + skip * x[:128]) * g_ref[:128, at]
        p_ref[128:, at] = (low + skip * x[128:]) * g_ref[128:, at]


def halves(core, mine_ref, other_ref):
    at = pl.ds(pl.multiple_of(core * HALF, HALF), HALF)
    mine, other = mine_ref[:1, at], other_ref[:1, at]
    return pick(core, mine, other), pick(core, other, mine)


def chip_state(keep_ref, came_ref, tot_ref, tot_other_ref, s0, s1, s2, s3, message):
    core = lax.axis_index("core")
    log0, log1 = halves(core, tot_ref, tot_other_ref)
    keep, came = keep_ref[...], came_ref[...].astype(F32)
    message[:STATE, :] = (
        jnp.exp(log1) * pick(core, keep, came) + pick(core, came, keep)
    ).astype(BF16)
    message[STATE:, :] = log_block(log0 + log1)
    for k, out in zip(ROUND_X, (s0, s1, s2, s3)):
        out[...] = message[:, pl.ds(pl.multiple_of(place("x", k, 4) * PART, PART), PART)]


def row_state(m0, m1, m2, m3, all_ref, row_ref):
    for k, piece in zip(ROUND_X, (m0, m1, m2, m3)):
        all_ref[place("x", -k, 4)] = piece[...]
    state = state_of(all_ref[0])
    logs = logs_of(all_ref[0])
    for x in range(1, 4):
        log = logs_of(all_ref[x])
        state = jnp.exp(log) * state + state_of(all_ref[x])
        logs = logs + log
    row_ref[:STATE, :] = state.astype(BF16)
    row_ref[STATE:, :] = log_block(logs)


def four_rows(r0, r1, r2, r3, inner_ref, logs_ref, total_ref, rows):
    for k, piece in enumerate((r0, r1, r2, r3)):
        rows[lax.rem(lax.axis_index("z") + 4 - k, 4)] = piece[...]
    me = lax.rem(lax.axis_index("z"), 4)
    state, logs = state_of(rows[0]), logs_of(rows[0])
    inner, before = jnp.zeros_like(state), jnp.zeros_like(logs)
    for z in range(1, 4):
        inner, before = pick(me - z, state, inner), pick(me - z, logs, before)
        log = logs_of(rows[z])
        state = jnp.exp(log) * state + state_of(rows[z])
        logs = logs + log
    inner_ref[...] = inner
    logs_ref[...] = jnp.broadcast_to(before, (8, PART))
    total_ref[...] = state.astype(BF16)


def enter(inner_ref, logs_ref, far_ref, all_ref, e0, e1, e2, e3, every):
    state = jnp.exp(logs_ref[:1, :]) * pick(lax.div(lax.axis_index("z"), 4), jnp.zeros((STATE, PART), F32), far_ref[...].astype(F32)) + inner_ref[...]
    for x in range(4):
        every[x] = state.astype(BF16)
        if x < 3:
            state = jnp.exp(logs_of(all_ref[x])) * state + state_of(all_ref[x])
    for k, out in zip(ROUND_X, (e0, e1, e2, e3)):
        out[...] = every[place("x", k, 4)]


def core_states(f0, f1, f2, f3, keep_ref, came_ref, tot_ref, tot_other_ref, own_ref, give_ref, chip):
    for k, piece in zip(ROUND_X, (f0, f1, f2, f3)):
        chip[:, pl.ds(pl.multiple_of(place("x", -k, 4) * PART, PART), PART)] = piece[...]
    core = lax.axis_index("core")
    log0, _ = halves(core, tot_ref, tot_other_ref)
    first = chip[...].astype(F32)
    local = pick(core, keep_ref[...], came_ref[...].astype(F32))
    second = jnp.exp(log0) * first + local
    own_ref[...] = pick(core, first, second).astype(BF16)
    give_ref[...] = pick(core, second, first).astype(BF16)


def gate_all(own_ref, came_ref, c_ref, p_ref, q_ref, gated_ref, sums_ref, states):
    core = lax.axis_index("core")
    states[:, pl.ds(pl.multiple_of(core * HALF, HALF), HALF)] = own_ref[...]
    states[:, pl.ds(pl.multiple_of((1 - core) * HALF, HALF), HALF)] = came_ref[...]
    total = jnp.zeros((STRETCH, 128), F32)
    for at in range(0, FEATS, 256):
        carried = jnp.dot(c_ref[...], states[:, at:at + 256], preferred_element_type=F32)
        gated = p_ref[:, at:at + 256] + q_ref[:, at:at + 256] * carried
        gated_ref[:, at:at + 256] = gated
        square = gated * gated
        total = total + square[:, :128] + square[:, 128:]
    sums_ref[...] = jnp.broadcast_to(jnp.sum(total.T, axis=0, keepdims=True), (8, STRETCH))


def normalize(gated_ref, q0, q1, q2, q3, gain_ref, out_hbm, out_ref, sems):
    total = q0[:1, :] + q1[:1, :] + q2[:1, :] + q3[:1, :]
    scale = lax.rsqrt(total / (HEADS * HEAD_DIM) + epsilon)
    scale = jnp.broadcast_to(scale, (128, STRETCH)).T
    copies = []
    for k in range(4):
        rows = slice(k * 64, k * 64 + 64)
        for at in range(0, FEATS, 128):
            out_ref[rows, at:at + 128] = (
                gated_ref[rows, at:at + 128] * scale[rows] * gain_ref[:, at:at + 128]
            ).astype(BF16)
        copy = pltpu.make_async_copy(out_ref.at[rows], out_hbm.at[rows], sems.at[k])
        copy.start()
        copies.append(copy)
    for copy in copies:
        copy.wait()


def shifted(v, axis, step, size):
    return lax.ppermute(v, axis, [(i, (i + step) % size) for i in range(size)])


def triple(pieces, axis, steps):
    return [shifted(piece, axis, k, 4) for k, piece in zip(steps, pieces[1:])]


def on_device(inputs, gate, in_b, in_c, log_decay, step_size, importance, skip, norm_gain):
    y = lax.axis_index("head")
    pieces = [
        lax.dynamic_slice(inputs, (0, lax.rem(y + k, 4) * FEATS), (64, FEATS)) for k in ROUND_Y[1:]
    ]
    pieces = triple([inputs] + pieces, "head", ROUND_Y[1:])

    big = (STRETCH, FEATS)
    weights, dt, dtt, q, g, b_t, tot, skip_row = kernel_call(
        prepare,
        [((HERE, STRETCH, STRETCH), BF16), (big, F32), (big, F32), (big, F32), (big, F32),
         ((STATE, STRETCH), BF16), ((8, FEATS), F32), ((8, FEATS), F32)],
        log_decay, step_size, importance.reshape(1, STRETCH), skip.reshape(1, HERE),
        in_b, in_c, gate,
        flops=4 << 30, bytes_accessed=12 << 20,
    )
    tot_other = shifted(tot, "core", 1, 2)
    x, keep, send = kernel_call(
        end_state,
        [(big, BF16), ((STATE, HALF), F32), ((STATE, HALF), BF16)],
        inputs, *pieces, dtt, b_t,
        scratch=[((STATE, FEATS), F32)],
        after=[tot_other],
        flops=1 << 28, bytes_accessed=4 << 20,
    )
    came = shifted(send, "core", 1, 2)

    message = (STATE + LOGS, PART)
    slices = kernel_call(
        chip_state, [(message, BF16)] * 4, keep, came, tot, tot_other,
        scratch=[((STATE + LOGS, HALF), BF16)],
    )
    (p,) = kernel_call(
        inside, [(big, F32)], x, dt, weights, g, skip_row, after=[slices[0]],
        flops=2 << 30, bytes_accessed=11 << 20,
    )
    slices = [slices[0]] + triple(slices, "x", ROUND_X[1:])
    chips, row = kernel_call(
        row_state, [((4,) + message, BF16), (message, BF16)], *slices, after=[p]
    )
    near = [
        lax.ppermute(row, "z", [(i, i // 4 * 4 + (i + k) % 4) for i in range(8)]) for k in (1, 2, 3)
    ]
    inner, logs, total = kernel_call(
        four_rows, [((STATE, PART), F32), ((8, PART), F32), ((STATE, PART), BF16)], row, *near,
        scratch=[((4,) + message, BF16)],
    )
    far = lax.ppermute(total, "z", [(i, 7 - i) for i in range(8)])
    enters = kernel_call(
        enter, [((STATE, PART), BF16)] * 4, inner, logs, far, chips,
        scratch=[((4, STATE, PART), BF16)],
    )
    enters = [enters[0]] + triple(enters, "x", ROUND_X[1:])
    own, give = kernel_call(
        core_states, [((STATE, HALF), BF16)] * 2, *enters, keep, came, tot, tot_other,
        scratch=[((STATE, HALF), BF16)],
    )
    got = shifted(give, "core", 1, 2)
    gated, sums = kernel_call(
        gate_all, [(big, F32), ((8, STRETCH), F32)], own, got, in_c, p, q,
        scratch=[((STATE, FEATS), BF16)],
    )
    others = triple([sums] * 4, "head", (1, 2, 3))
    (out,) = kernel_call(
        normalize, [(big, BF16)], gated, sums, *others, norm_gain.reshape(1, FEATS),
        scratch=[(big, BF16)], hbm_out=True, copies=4,
    )
    return out


def solution(mesh):
    fine = Mesh(mesh.devices.reshape(8, 4, 2, 4), ("z", "x", "core", "head"))
    seq = ("z", "x", "core")
    in_specs = (
        P(seq + ("head",), None),
        P(seq, "head"),
        P(seq, None),
        P(seq, None),
        P("head", seq),
        P("head", seq),
        P(seq),
        P("head"),
        P("head"),
    )
    return jax.shard_map(
        on_device, mesh=fine, in_specs=in_specs, out_specs=P(seq, "head"), check_vma=False
    )
```

```python
import functools

import jax
import jax.numpy as jnp
from jax import lax
from jax.experimental import pallas as pl
from jax.experimental.pallas import tpu as pltpu
from jax.sharding import Mesh, PartitionSpec as P

HEADS = 128
HEAD_DIM = 64
STATE = 128
STRETCH = 256
epsilon = 1e-05

F32 = jnp.float32
BF16 = jnp.bfloat16
HERE = 32
FEATS = HERE * HEAD_DIM
HALF = FEATS // 2
PART = HALF // 4
ROUND_Y = (0, 3, 2, 1)
ROUND_X = (0, 1, 2, 3)
LOGS = 16


def kernel_call(body, outs, *args, scratch=(), after=(), flops=0, bytes_accessed=0,
                hbm_in=False, hbm_out=False, copies=0):
    vmem, hbm = pl.BlockSpec(memory_space=pltpu.VMEM), pl.BlockSpec(memory_space=pltpu.HBM)
    count = len(args)

    def ordered(*refs):
        body(*refs[:count], *refs[count + len(after):])

    return pl.pallas_call(
        ordered,
        out_shape=[jax.ShapeDtypeStruct(s, d) for s, d in outs],
        in_specs=[hbm if hbm_in else vmem] * count
        + [pl.BlockSpec(memory_space=pl.ANY)] * len(after),
        out_specs=[hbm if hbm_out else vmem] * len(outs),
        scratch_shapes=[pltpu.VMEM(s, d) for s, d in scratch]
        + ([pltpu.SemaphoreType.DMA((copies,))] if copies else []),
        compiler_params=pltpu.CompilerParams(vmem_limit_bytes=20 * 1024 * 1024),
        cost_estimate=pl.CostEstimate(
            flops=flops, bytes_accessed=bytes_accessed, transcendentals=0
        ),
    )(*args, *after)


def three_terms(v):
    hi = v.astype(BF16).astype(F32)
    rest = v - hi
    mid = rest.astype(BF16).astype(F32)
    return hi, mid, rest - mid


def pick(index, first, second):
    return jnp.where(jnp.full(first.shape, index, jnp.int32) == 0, first, second)


def place(axis, step, size):
    return lax.rem(lax.axis_index(axis) + (step + size), size)


def log_block(row):
    hi, mid, lo = three_terms(row)
    at = lax.broadcasted_iota(jnp.int32, (LOGS, row.shape[1]), 0)
    return jnp.where(at == 0, hi, jnp.where(at == 1, mid, jnp.where(at == 2, lo, 0.0))).astype(BF16)


def logs_of(message):
    block = message[STATE:, :].astype(F32)
    return jnp.sum(block[:8, :], axis=0, keepdims=True)


def state_of(message):
    return message[:STATE, :].astype(F32)


def prepare(log_ref, step_ref, imp_ref, skip_ref, b_ref, c_ref, gate_ref,
            w_ref, dt_ref, dtt_ref, q_ref, g_ref, bt_ref, tot_ref, skip_row_ref):
    lane = lax.broadcasted_iota(jnp.int32, (HERE, STRETCH), 1)
    cum = log_ref[...]
    shift = 1
    while shift < STRETCH:
        cum = cum + jnp.where(lane >= shift, pltpu.roll(cum, shift, 1), 0.0)
        shift *= 2
    step = step_ref[...] * imp_ref[...]
    tail = jnp.exp(cum[:, STRETCH - 1:] - cum)
    spread = (
        lax.broadcasted_iota(jnp.int32, (128, FEATS), 0) % HERE
        == lax.broadcasted_iota(jnp.int32, (128, FEATS), 1) // HEAD_DIM
    ).astype(F32).astype(BF16)
    blank = jnp.zeros((HERE, STRETCH), F32)

    def columns(v):
        hi, mid, lo = three_terms(v)
        return jnp.concatenate([hi, mid, lo, blank], axis=0).T.astype(BF16)

    def expand(v, into):
        for at in range(0, FEATS, 512):
            into(at, jnp.dot(v, spread[:, at:at + 512], preferred_element_type=F32))

    def put_dt(at, v):
        dt_ref[:, at:at + 512] = v

    def put_dtt(at, v):
        dtt_ref[:, at:at + 512] = v

    def put_gate(at, v):
        gate = gate_ref[:, at:at + 512].astype(F32)
        g = gate / (1.0 + jnp.exp(-gate))
        g_ref[:, at:at + 512] = g
        q_ref[:, at:at + 512] = v * g

    expand(columns(step), put_dt)
    expand(columns(step * tail), put_dtt)
    expand(columns(jnp.exp(cum)), put_gate)
    logs = columns(cum)
    last = jnp.broadcast_to(logs[STRETCH - 16:, :][15:, :], (16, 128))
    tot_ref[...] = jnp.dot(last, spread, preferred_element_type=F32)[:8]
    hi, mid, lo = three_terms(jnp.broadcast_to(skip_ref[...], (16, HERE)))
    skip = jnp.concatenate([hi, mid, lo, jnp.zeros_like(hi)], axis=1).astype(BF16)
    skip_row_ref[...] = jnp.dot(skip, spread, preferred_element_type=F32)[:8]
    bt_ref[...] = b_ref[...].astype(F32).T.astype(BF16)

    scores = lax.dot_general(
        c_ref[...], b_ref[...], (((1,), (1,)), ((), ())), preferred_element_type=F32
    )
    cum_columns = jnp.concatenate([cum, blank, blank, blank], axis=0).T
    tri = (
        lax.broadcasted_iota(jnp.int32, (128, 128), 0)
        >= lax.broadcasted_iota(jnp.int32, (128, 128), 1)
    )
    for h in range(HERE):
        row = cum[h:h + 1, :]
        top = cum_columns[:128, h:h + 1]
        low = cum_columns[128:, h:h + 1]
        w_ref[h, :128, :128] = (
            jnp.exp(jnp.where(tri, top - row[:, :128], -1e30)) * scores[:128, :128]
        ).astype(BF16)
        w_ref[h, 128:, :128] = (jnp.exp(low - row[:, :128]) * scores[128:, :128]).astype(BF16)
        w_ref[h, 128:, 128:] = (
            jnp.exp(jnp.where(tri, low - row[:, 128:], -1e30)) * scores[128:, 128:]
        ).astype(BF16)


def end_state(all_ref, x1, x2, x3, dtt_ref, bt_ref, x_ref, keep_ref, send_ref, local):
    y = lax.axis_index("head")
    own = pl.ds(pl.multiple_of(y * FEATS, FEATS), FEATS)
    x_ref[pl.ds(pl.multiple_of(y * 64, 64), 64), :] = all_ref[:, own]
    for k, piece in zip(ROUND_Y[1:], (x1, x2, x3)):
        at = pl.multiple_of(place("head", -k, 4) * 64, 64)
        x_ref[pl.ds(at, 64), :] = piece[...]
    for at in range(0, FEATS, 256):
        decayed = (x_ref[:, at:at + 256].astype(F32) * dtt_ref[:, at:at + 256]).astype(BF16)
        local[:, at:at + 256] = jnp.dot(bt_ref[...], decayed, preferred_element_type=F32)
    core = lax.axis_index("core")
    keep_ref[...] = local[:, pl.ds(pl.multiple_of(core * HALF, HALF), HALF)]
    send_ref[...] = local[:, pl.ds(pl.multiple_of((1 - core) * HALF, HALF), HALF)].astype(BF16)


def inside(x_ref, dt_ref, w_ref, g_ref, skip_ref, p_ref):
    first = lax.broadcasted_iota(jnp.int32, (STRETCH, 128), 1) < HEAD_DIM
    for j in range(FEATS // 128):
        at = slice(j * 128, j * 128 + 128)
        x = x_ref[:, at].astype(F32)
        scaled = x * dt_ref[:, at]
        one = jnp.where(first, scaled, 0.0).astype(BF16)
        two = jnp.where(first, 0.0, scaled).astype(BF16)
        top = jnp.dot(w_ref[2 * j, :128, :128], one[:128], preferred_element_type=F32)
        top += jnp.dot(w_ref[2 * j + 1, :128, :128], two[:128], preferred_element_type=F32)
        low = jnp.dot(w_ref[2 * j, 128:, :], one, preferred_element_type=F32)
        low += jnp.dot(w_ref[2 * j + 1, 128:, :], two, preferred_element_type=F32)
        skip = skip_ref[:1, at]
        p_ref[:128, at] = (top + skip * x[:128]) * g_ref[:128, at]
        p_ref[128:, at] = (low + skip * x[128:]) * g_ref[128:, at]


def halves(core, mine_ref, other_ref):
    at = pl.ds(pl.multiple_of(core * HALF, HALF), HALF)
    mine, other = mine_ref[:1, at], other_ref[:1, at]
    return pick(core, mine, other), pick(core, other, mine)


def chip_state(keep_ref, came_ref, tot_ref, tot_other_ref, s0, s1, s2, s3, message):
    core = lax.axis_index("core")
    log0, log1 = halves(core, tot_ref, tot_other_ref)
    keep, came = keep_ref[...], came_ref[...].astype(F32)
    message[:STATE, :] = (
        jnp.exp(log1) * pick(core, keep, came) + pick(core, came, keep)
    ).astype(BF16)
    message[STATE:, :] = log_block(log0 + log1)
    for k, out in zip(ROUND_X, (s0, s1, s2, s3)):
        out[...] = message[:, pl.ds(pl.multiple_of(place("x", k, 4) * PART, PART), PART)]


def row_state(m0, m1, m2, m3, all_ref, row_ref):
    for k, piece in zip(ROUND_X, (m0, m1, m2, m3)):
        all_ref[place("x", -k, 4)] = piece[...]
    state = state_of(all_ref[0])
    logs = logs_of(all_ref[0])
    for x in range(1, 4):
        log = logs_of(all_ref[x])
        state = jnp.exp(log) * state + state_of(all_ref[x])
        logs = logs + log
    row_ref[:STATE, :] = state.astype(BF16)
    row_ref[STATE:, :] = log_block(logs)


def four_rows(r0, r1, r2, r3, inner_ref, logs_ref, total_ref, rows):
    for k, piece in enumerate((r0, r1, r2, r3)):
        rows[lax.rem(lax.axis_index("z") + 4 - k, 4)] = piece[...]
    me = lax.rem(lax.axis_index("z"), 4)
    state, logs = state_of(rows[0]), logs_of(rows[0])
    inner, before = jnp.zeros_like(state), jnp.zeros_like(logs)
    for z in range(1, 4):
        inner, before = pick(me - z, state, inner), pick(me - z, logs, before)
        log = logs_of(rows[z])
        state = jnp.exp(log) * state + state_of(rows[z])
        logs = logs + log
    inner_ref[...] = inner
    logs_ref[...] = jnp.broadcast_to(before, (8, PART))
    total_ref[...] = state.astype(BF16)


def enter(inner_ref, logs_ref, far_ref, all_ref, e0, e1, e2, e3, every):
    state = jnp.exp(logs_ref[:1, :]) * pick(lax.div(lax.axis_index("z"), 4), jnp.zeros((STATE, PART), F32), far_ref[...].astype(F32)) + inner_ref[...]
    for x in range(4):
        every[x] = state.astype(BF16)
        if x < 3:
            state = jnp.exp(logs_of(all_ref[x])) * state + state_of(all_ref[x])
    for k, out in zip(ROUND_X, (e0, e1, e2, e3)):
        out[...] = every[place("x", k, 4)]


def core_states(f0, f1, f2, f3, keep_ref, came_ref, tot_ref, tot_other_ref, own_ref, give_ref, chip):
    for k, piece in zip(ROUND_X, (f0, f1, f2, f3)):
        chip[:, pl.ds(pl.multiple_of(place("x", -k, 4) * PART, PART), PART)] = piece[...]
    core = lax.axis_index("core")
    log0, _ = halves(core, tot_ref, tot_other_ref)
    first = chip[...].astype(F32)
    local = pick(core, keep_ref[...], came_ref[...].astype(F32))
    second = jnp.exp(log0) * first + local
    own_ref[...] = pick(core, first, second).astype(BF16)
    give_ref[...] = pick(core, second, first).astype(BF16)


def gate_all(own_ref, came_ref, c_ref, p_ref, q_ref, gated_ref, sums_ref, states):
    core = lax.axis_index("core")
    states[:, pl.ds(pl.multiple_of(core * HALF, HALF), HALF)] = own_ref[...]
    states[:, pl.ds(pl.multiple_of((1 - core) * HALF, HALF), HALF)] = came_ref[...]
    total = jnp.zeros((STRETCH, 128), F32)
    for at in range(0, FEATS, 256):
        carried = jnp.dot(c_ref[...], states[:, at:at + 256], preferred_element_type=F32)
        gated = p_ref[:, at:at + 256] + q_ref[:, at:at + 256] * carried
        gated_ref[:, at:at + 256] = gated
        square = gated * gated
        total = total + square[:, :128] + square[:, 128:]
    sums_ref[...] = jnp.broadcast_to(jnp.sum(total.T, axis=0, keepdims=True), (8, STRETCH))


def normalize(gated_ref, q0, q1, q2, q3, gain_ref, out_hbm, out_ref, sems):
    total = q0[:1, :] + q1[:1, :] + q2[:1, :] + q3[:1, :]
    scale = lax.rsqrt(total / (HEADS * HEAD_DIM) + epsilon)
    scale = jnp.broadcast_to(scale, (128, STRETCH)).T
    copies = []
    for k in range(4):
        rows = slice(k * 64, k * 64 + 64)
        for at in range(0, FEATS, 128):
            out_ref[rows, at:at + 128] = (
                gated_ref[rows, at:at + 128] * scale[rows] * gain_ref[:, at:at + 128]
            ).astype(BF16)
        copy = pltpu.make_async_copy(out_ref.at[rows], out_hbm.at[rows], sems.at[k])
        copy.start()
        copies.append(copy)
    for copy in copies:
        copy.wait()


def shifted(v, axis, step, size):
    return lax.ppermute(v, axis, [(i, (i + step) % size) for i in range(size)])


def triple(pieces, axis, steps):
    return [shifted(piece, axis, k, 4) for k, piece in zip(steps, pieces[1:])]


def on_device(inputs, gate, in_b, in_c, log_decay, step_size, importance, skip, norm_gain):
    y = lax.axis_index("head")
    pieces = [
        lax.dynamic_slice(inputs, (0, lax.rem(y + k, 4) * FEATS), (64, FEATS)) for k in ROUND_Y[1:]
    ]
    pieces = triple([inputs] + pieces, "head", ROUND_Y[1:])

    big = (STRETCH, FEATS)
    weights, dt, dtt, q, g, b_t, tot, skip_row = kernel_call(
        prepare,
        [((HERE, STRETCH, STRETCH), BF16), (big, F32), (big, F32), (big, F32), (big, F32),
         ((STATE, STRETCH), BF16), ((8, FEATS), F32), ((8, FEATS), F32)],
        log_decay, step_size, importance.reshape(1, STRETCH), skip.reshape(1, HERE),
        in_b, in_c, gate,
        flops=4 << 30, bytes_accessed=12 << 20,
    )
    tot_other = shifted(tot, "core", 1, 2)
    x, keep, send = kernel_call(
        end_state,
        [(big, BF16), ((STATE, HALF), F32), ((STATE, HALF), BF16)],
        inputs, *pieces, dtt, b_t,
        scratch=[((STATE, FEATS), F32)],
        after=[tot_other],
        flops=1 << 28, bytes_accessed=4 << 20,
    )
    came = shifted(send, "core", 1, 2)

    message = (STATE + LOGS, PART)
    slices = kernel_call(
        chip_state, [(message, BF16)] * 4, keep, came, tot, tot_other,
        scratch=[((STATE + LOGS, HALF), BF16)],
    )
    (p,) = kernel_call(
        inside, [(big, F32)], x, dt, weights, g, skip_row, after=[slices[0]],
        flops=2 << 30, bytes_accessed=11 << 20,
    )
    slices = [slices[0]] + triple(slices, "x", ROUND_X[1:])
    chips, row = kernel_call(
        row_state, [((4,) + message, BF16), (message, BF16)], *slices, after=[p]
    )
    near = [
        lax.ppermute(row, "z", [(i, i // 4 * 4 + (i + k) % 4) for i in range(8)]) for k in (1, 2, 3)
    ]
    inner, logs, total = kernel_call(
        four_rows, [((STATE, PART), F32), ((8, PART), F32), ((STATE, PART), BF16)], row, *near,
        scratch=[((4,) + message, BF16)],
    )
    far = lax.ppermute(total, "z", [(i, 7 - i) for i in range(8)])
    enters = kernel_call(
        enter, [((STATE, PART), BF16)] * 4, inner, logs, far, chips,
        scratch=[((4, STATE, PART), BF16)],
    )
    enters = [enters[0]] + triple(enters, "x", ROUND_X[1:])
    own, give = kernel_call(
        core_states, [((STATE, HALF), BF16)] * 2, *enters, keep, came, tot, tot_other,
        scratch=[((STATE, HALF), BF16)],
    )
    got = shifted(give, "core", 1, 2)
    gated, sums = kernel_call(
        gate_all, [(big, F32), ((8, STRETCH), F32)], own, got, in_c, p, q,
        scratch=[((STATE, FEATS), BF16)],
    )
    others = triple([sums] * 4, "head", (1, 2, 3))
    (out,) = kernel_call(
        normalize, [(big, BF16)], gated, sums, *others, norm_gain.reshape(1, FEATS),
        scratch=[(big, BF16)], hbm_out=True, copies=4,
    )
    return out


def solution(mesh):
    fine = Mesh(mesh.devices.reshape(8, 4, 2, 4), ("z", "x", "core", "head"))
    seq = ("z", "x", "core")
    in_specs = (
        P(seq + ("head",), None),
        P(seq, "head"),
        P(seq, None),
        P(seq, None),
        P("head", seq),
        P("head", seq),
        P(seq),
        P("head"),
        P("head"),
    )
    return jax.shard_map(
        on_device, mesh=fine, in_specs=in_specs, out_specs=P(seq, "head"), check_vma=False
    )
```
